1024 devices in a mesh: expert: 32 (over y, x, core), dp: 32 (over z).
Axes of the slice: x: 4, y: 4, z: 32, core: 2. Of those that a mesh axis runs over, the one named last changes fastest.
Arguments:
- grad_out: bfloat16 [1024, 7168], P('expert', 'dp'), may hold values from -6 to 6
- expert_ids: int32 [1024, 8], P('expert'), may hold values from 0 to 31, all different within a row; in each aligned block of 32 rows (0 to 31, 32 to 63, ...) at most 12 rows name the same one
- gate_weights: float32 [1024, 8], P('expert'), may hold values from 0.05 to 0.5
- layer_inputs: bfloat16 [1024, 7168], P('expert', 'dp'), may hold values from -6 to 6
- shared_pre: bfloat16 [1024, 2048], P('expert'), may hold values from -6 to 6
- routed_inputs: bfloat16 [32, 384, 7168], P('expert', None, 'dp'), may hold values from -6 to 6
- routed_pre: bfloat16 [32, 384, 2048], P('expert'), may hold values from -6 to 6
- w_gate_up: bfloat16 [32, 7168, 2048], P('expert', 'dp'), may hold values from -0.125 to 0.125
- w_down: bfloat16 [32, 1024, 7168], P('expert', None, 'dp'), may hold values from -0.0625 to 0.0625
- shared_gate_up: bfloat16 [7168, 2048], P('dp'), may hold values from -0.125 to 0.125
- shared_down: bfloat16 [1024, 7168], P(None, 'dp'), may hold values from -0.0625 to 0.0625
Outputs:
- grad_in: bfloat16 [1024, 7168], P('expert', 'dp')
- grad_gate_up: bfloat16 [32, 7168, 2048], P('expert', 'dp')
- grad_down: bfloat16 [32, 1024, 7168], P('expert', None, 'dp')
- shared_grad_gate_up: bfloat16 [7168, 2048], P('dp', 'expert')
- shared_grad_down: bfloat16 [1024, 7168], P('expert', 'dp')
The draws below stay inside these ranges and needn't reach their ends.
Inputs may be any that keep to these rules, and one draw needn't show every extreme that they name: `expert_ids`: among the 32 tokens of one block, each expert is named by at most 12 of them, a bound that some block reaches; a token names 8 different experts.
All inputs are finite; a program needn't handle non-finite values.
Results may differ from the reference program's by a relative error of at most 0.0057.
Values may be sent and summed in bfloat16 or wider, within the bound.
No kernel may reach another device: no remote copies, remote signals or barrier semaphores. Data moves between devices by JAX's collectives and lax.ppermute only.
A program may use at most 32 MiB of HBM per device.

```python
import math
import jax
import jax.numpy as jnp
import numpy as np
from jax import lax

D = 7168
H = 1024
HS = 1024
TOPK = 8
TOK_DEV = 32
EXPERTS = 32
CAP = 12
SLOTS = 384
TOKENS = 1024
N_EXPERT = 32


def levels(own_key, dims, split, smallest, high):
    level, own = 1.0, jax.random.fold_in(own_key, 6)
    for position, shards_of in split:
        steps = jnp.exp(jax.random.uniform(jax.random.fold_in(own, position), (shards_of,), jnp.float32, smallest / len(split), high / len(split)))
        level = level * jnp.repeat(steps, dims[position] // shards_of).reshape([-1 if axis == position else 1 for axis in range(len(dims))])
    return level


def routed_block(rng, own, number, rows, count, top, most, slope):
    order = jax.random.permutation(rng, count)
    crowded, common = portions_of(count, rows * top, most, slope, True), portions_of(count, rows * top, most, slope, False)
    places = jnp.arange(count)

    def named(tallies, turn):
        used = int((tallies > 0).sum())
        fixed = max(1, used // 4)
        moved = fixed + (places - fixed + turn * (used - fixed)) % max(1, count - fixed)
        return jnp.zeros((count,), jnp.int32).at[order[jnp.where(places < fixed, places, moved)]].set(jnp.asarray(tallies, jnp.int32))

    tallies = jnp.where(number % 4 == 0, named(crowded, number // 4), named(common, number - number // 4 - 1))
    mixed = jax.random.permutation(jax.random.fold_in(own, 3), count)
    source_of, taker = mixed[0:count // 2 * 2:2], mixed[1:count // 2 * 2:2]
    room = jnp.minimum(tallies[source_of] - 1, most - tallies[taker]) // 2
    room = jnp.where((source_of == order[0]) | (taker == order[0]) | (tallies[taker] == 0), 0, jnp.maximum(room, 0))
    moved = jax.random.randint(jax.random.fold_in(own, 4), (count // 2,), 0, 1 << 20) % (room + 1)
    tallies = tallies.at[source_of].add(-moved).at[taker].add(moved)
    members = jnp.searchsorted(jnp.cumsum(tallies), jnp.arange(rows * top), side="right").astype(jnp.int32)
    listing = members.reshape(top, rows).T
    listing = listing[jax.random.permutation(jax.random.fold_in(own, 1), rows)]
    turn = jax.random.randint(jax.random.fold_in(own, 2), (rows, 1), 0, top)
    return jnp.take_along_axis(listing, (jnp.arange(top)[None, :] + turn) % top, axis=1)


def portions_of(count, total, bound, slope, full):
    loads = [(1 << 20) // math.isqrt(rank ** slope) + 1 for rank in range(1, count + 1)]
    largest = bound if full else min(bound, max(-(-total // count), total * loads[0] // sum(loads)))
    least = 1 if total - largest >= count - 1 else 0
    counts, spare = [largest] + [least] * (count - 1), total - largest - least * (count - 1)
    while spare > 0:
        candidates = [i for i in range(1, count) if counts[i] < largest] or [i for i in range(1, count) if counts[i] < bound]
        mass, left = sum([loads[i] for i in candidates]), spare
        for i in candidates:
            extra = min(bound - counts[i], max(1, left * loads[i] // mass), spare)
            counts[i] = counts[i] + extra
            spare = spare - extra
    return np.array(counts)


def scatter_about(key, extent, width, bound, shards=(), kind=jnp.bfloat16):
    result = width * jax.random.normal(key, extent, jnp.float32)
    if shards:
        result = result * levels(key, extent, shards, -0.22, 0.18)
    return jnp.clip(result, -bound, bound).astype(kind)


def setup_inputs(seed: int = 0) -> dict:
    arg_keys = jax.random.split(jax.random.key(seed), 12)
    grad_out = scatter_about(arg_keys[0], (TOKENS, D), 1.0, 6.0, ((0, 32), (1, 32)))
    expert_ids_keys = jax.random.split(jax.random.fold_in(arg_keys[1], 1), TOKENS // TOK_DEV)
    expert_ids_turns = jax.random.permutation(jax.random.fold_in(arg_keys[1], 3), TOKENS // TOK_DEV)
    expert_ids = jax.vmap(lambda own, number: routed_block(jax.random.fold_in(arg_keys[1], 2), own, number, TOK_DEV, EXPERTS, TOPK, CAP, 2))(expert_ids_keys, expert_ids_turns).reshape((TOKENS, TOPK))
    gate_weights = jnp.clip(jnp.exp(math.log(0.5) - 2.3025851 * jax.random.uniform(arg_keys[2], (TOKENS, TOPK), jnp.float32) ** levels(arg_keys[2], (TOKENS, TOPK), ((0, 32),), -0.2, 0.2)), 0.05, 0.5)
    layer_inputs = scatter_about(arg_keys[3], (TOKENS, D), 1.0, 6.0, ((0, 32), (1, 32)))
    shared_pre = scatter_about(arg_keys[4], (TOKENS, 2 * HS), 1.5, 6.0, ((0, 32),))
    routed_inputs = scatter_about(arg_keys[5], (EXPERTS, SLOTS, D), 1.0, 6.0, ((0, 32), (2, 32)))
    routed_pre = scatter_about(arg_keys[6], (EXPERTS, SLOTS, 2 * H), 1.5, 6.0, ((0, 32),))
    w_gate_up = scatter_about(arg_keys[7], (EXPERTS, D, 2 * H), (2 * H) ** -0.5, 0.125, ((0, 32), (1, 32)))
    w_down = scatter_about(arg_keys[8], (EXPERTS, H, D), D ** -0.5, 0.0625, ((0, 32), (2, 32)))
    shared_gate_up = scatter_about(arg_keys[9], (D, 2 * HS), (2 * HS) ** -0.5, 0.125, ((0, 32),))
    shared_down = scatter_about(arg_keys[10], (HS, D), D ** -0.5, 0.0625, ((1, 32),))
    return dict(grad_out=grad_out, expert_ids=expert_ids, gate_weights=gate_weights, layer_inputs=layer_inputs, shared_pre=shared_pre, routed_inputs=routed_inputs, routed_pre=routed_pre, w_gate_up=w_gate_up, w_down=w_down, shared_gate_up=shared_gate_up, shared_down=shared_down)


def swiglu_terms(gate_pre, up_pre, grad_hidden):
    sigmoid_gate = jax.nn.sigmoid(gate_pre)
    activated = gate_pre * sigmoid_gate
    grad_gate = grad_hidden * up_pre * sigmoid_gate * (1.0 + gate_pre * (1.0 - sigmoid_gate))
    return grad_gate, grad_hidden * activated, activated * up_pre


def slot_table(expert_ids):
    flat_ids = expert_ids.reshape(N_EXPERT, TOK_DEV * TOPK).astype(jnp.int32)
    onehot = (flat_ids[:, :, None] == jnp.arange(EXPERTS, dtype=jnp.int32)[None, None, :]).astype(jnp.int32)
    before = (jnp.cumsum(onehot, axis=1) - onehot).astype(jnp.int32)
    slot_rank = jnp.sum(before * onehot, axis=2).astype(jnp.int32)
    source = jnp.arange(N_EXPERT, dtype=jnp.int32)[:, None]
    return (flat_ids * SLOTS + source * CAP + slot_rank).reshape(TOKENS * TOPK).astype(jnp.int32)


def expert_back(operands):
    route_rows, inputs, saved_pre, weight_gate_up, weight_down = operands
    grad_hidden = jnp.dot(route_rows, weight_down.T, preferred_element_type=jnp.float32)
    grad_gate, grad_up, hidden_value = swiglu_terms(saved_pre[:, :H].astype(jnp.float32), saved_pre[:, H:].astype(jnp.float32), grad_hidden)
    grad_pre = jnp.concatenate([grad_gate, grad_up], axis=1).astype(jnp.bfloat16)
    hidden = hidden_value.astype(jnp.bfloat16)
    grad_down = jnp.dot(hidden.T, route_rows, preferred_element_type=jnp.float32).astype(jnp.bfloat16)
    grad_gate_up = jnp.dot(inputs.T, grad_pre, preferred_element_type=jnp.float32).astype(jnp.bfloat16)
    returned = jnp.dot(grad_pre, weight_gate_up.T, preferred_element_type=jnp.float32).astype(jnp.bfloat16)
    return returned, grad_gate_up, grad_down


def reference(grad_out, expert_ids, gate_weights, layer_inputs, shared_pre, routed_inputs, routed_pre, w_gate_up, w_down, shared_gate_up, shared_down):
    slot_index = slot_table(expert_ids)
    scaled = (gate_weights[:, :, None] * grad_out[:, None, :].astype(jnp.float32)).astype(jnp.bfloat16)
    dispatched = jnp.zeros((EXPERTS * SLOTS, D), jnp.bfloat16).at[slot_index].set(scaled.reshape(TOKENS * TOPK, D))
    dispatched = dispatched.reshape(EXPERTS, SLOTS, D)
    returned, grad_gate_up, grad_down = lax.map(expert_back, (dispatched, routed_inputs, routed_pre, w_gate_up, w_down))
    picked = returned.reshape(EXPERTS * SLOTS, D)[slot_index].reshape(TOKENS, TOPK, D)
    routed_sum = jnp.sum(picked.astype(jnp.float32), axis=1)
    shared_hidden_grad = jnp.dot(grad_out, shared_down.T, preferred_element_type=jnp.float32)
    shared_gate, shared_up, shared_value = swiglu_terms(shared_pre[:, :HS].astype(jnp.float32), shared_pre[:, HS:].astype(jnp.float32), shared_hidden_grad)
    shared_pre_grad = jnp.concatenate([shared_gate, shared_up], axis=1).astype(jnp.bfloat16)
    shared_hidden = shared_value.astype(jnp.bfloat16)
    shared_grad_down = jnp.dot(shared_hidden.T, grad_out, preferred_element_type=jnp.float32).astype(jnp.bfloat16)
    shared_grad_gate_up = jnp.dot(layer_inputs.T, shared_pre_grad, preferred_element_type=jnp.float32).astype(jnp.bfloat16)
    shared_back = jnp.dot(shared_pre_grad, shared_gate_up.T, preferred_element_type=jnp.float32)
    grad_in = (shared_back + routed_sum).astype(jnp.bfloat16)
    return grad_in, grad_gate_up, grad_down, shared_grad_gate_up, shared_grad_down
```

```python
import jax
import jax.numpy as jnp
from jax import lax
from jax.experimental import pallas as pl
from jax.experimental.pallas import tpu as pltpu
from jax.sharding import PartitionSpec as P

NEAR = 4


def route_kernel(capacity, ids_ref, gates_ref, grad_ref, sel_ref, out_ref):
    slots, tokens = sel_ref.shape
    slot = lax.broadcasted_iota(jnp.int32, (slots, 1), 0)
    expert = slot // capacity
    place = (slot - expert * capacity).astype(jnp.float32)
    ids = ids_ref[...]
    gates = gates_ref[...]
    hit = jnp.zeros((slots, tokens), jnp.float32)
    weight = jnp.zeros((slots, tokens), jnp.float32)
    for k in range(ids.shape[0]):
        same = ids[k : k + 1, :] == expert
        hit = jnp.where(same, 1.0, hit)
        weight = jnp.where(same, gates[k : k + 1, :], weight)
    row = lax.broadcasted_iota(jnp.int32, (tokens, tokens), 0)
    col = lax.broadcasted_iota(jnp.int32, (tokens, tokens), 1)
    earlier = jnp.where(row < col, 1.0, 0.0).astype(jnp.bfloat16)
    rank = jnp.dot(hit.astype(jnp.bfloat16), earlier, preferred_element_type=jnp.float32)
    taken = (hit > 0.0) & (rank == place)
    sel = jnp.where(taken, 1.0, 0.0).astype(jnp.bfloat16)
    gate = jnp.sum(jnp.where(taken, weight, 0.0), axis=1, keepdims=True)
    rows = jnp.dot(sel, grad_ref[...], preferred_element_type=jnp.float32)
    sel_ref[...] = sel
    out_ref[...] = (gate * rows).astype(jnp.bfloat16)


def swiglu_back(saved_pre, grad_hidden):
    half = saved_pre.shape[-1] // 2
    gate = saved_pre[:, :half].astype(jnp.float32)
    up = saved_pre[:, half:].astype(jnp.float32)
    sig = jax.nn.sigmoid(gate)
    act = gate * sig
    d_gate = grad_hidden * up * sig * (1.0 + gate * (1.0 - sig))
    d_up = grad_hidden * act
    grad_pre = jnp.concatenate([d_gate, d_up], axis=1).astype(jnp.bfloat16)
    return grad_pre, (act * up).astype(jnp.bfloat16)


def dot(a, b, ca, cb):
    return lax.dot_general(a, b, (((ca,), (cb,)), ((), ())), preferred_element_type=jnp.float32)


def total(parts):
    acc = parts[0].astype(jnp.float32)
    for i in range(1, parts.shape[0]):
        acc = acc + parts[i].astype(jnp.float32)
    return acc.astype(jnp.bfloat16)


def on_device(
    grad_out,
    expert_ids,
    gate_weights,
    layer_inputs,
    shared_pre,
    routed_inputs,
    routed_pre,
    w_gate_up,
    w_down,
    shared_gate_up,
    shared_down,
):
    groups = lax.axis_size("expert")
    ring = lax.axis_size("dp")
    far = ring // NEAR
    near_groups = [[NEAR * a + b for b in range(NEAR)] for a in range(far)]
    far_groups = [[NEAR * a + b for a in range(far)] for b in range(NEAR)]
    slots = routed_pre.shape[1]
    capacity = slots // groups
    tokens, width = grad_out.shape
    hidden_width = w_down.shape[1]
    routed_pre, routed_inputs = routed_pre[0], routed_inputs[0]
    w_gate_up, w_down = w_gate_up[0], w_down[0]

    pad = jnp.zeros((tokens, 512 - 2 * width), jnp.bfloat16)
    everyone = lax.all_gather(
        jnp.concatenate([grad_out, layer_inputs, pad], axis=1), "expert", axis=0, tiled=True
    )

    sel, outgoing = pl.pallas_call(
        lambda *refs: route_kernel(capacity, *refs),
        out_shape=(
            jax.ShapeDtypeStruct((slots, tokens), jnp.bfloat16),
            jax.ShapeDtypeStruct((slots, width), jnp.bfloat16),
        ),
        name="route",
    )(expert_ids.T, gate_weights.T, grad_out)
    arrived = lax.all_to_all(
        outgoing.reshape(groups, capacity, width), "expert", split_axis=0, concat_axis=0, tiled=True
    ).reshape(slots, width)

    part = jnp.concatenate(
        [dot(arrived, w_down, 1, 1), dot(grad_out, shared_down, 1, 1)], axis=0
    ).astype(jnp.bfloat16)
    rows = (slots + tokens) // NEAR
    cols = hidden_width // far
    near = lax.all_to_all(
        part.reshape(NEAR, rows, hidden_width),
        "dp",
        split_axis=0,
        concat_axis=0,
        tiled=True,
        axis_index_groups=near_groups,
    )
    near = total(near)
    near = near.reshape(rows, far, cols).transpose(1, 0, 2)
    distant = lax.all_to_all(
        near,
        "dp",
        split_axis=0,
        concat_axis=0,
        tiled=True,
        axis_index_groups=far_groups,
    )
    own = total(distant)
    full = lax.all_gather(own, "dp", axis=0, tiled=False)
    full = full.reshape(far, NEAR, rows, cols).transpose(1, 2, 0, 3)
    full = full.reshape(slots + tokens, hidden_width).astype(jnp.float32)

    routed_grad, hidden = swiglu_back(routed_pre, full[:slots])
    shared_grad, shared_hidden = swiglu_back(shared_pre, full[slots:])

    lanes = 128
    returned = dot(routed_grad, w_gate_up, 1, 1).astype(jnp.bfloat16)
    low = returned[:, :lanes].reshape(groups, capacity, lanes)
    high = jnp.pad(returned[:, lanes:], ((0, 0), (0, 2 * lanes - width)))
    high = high.reshape(groups, capacity, lanes)
    gu_cols = 2 * hidden_width // groups
    down_cols = hidden_width // groups
    shared_cols = jnp.concatenate(
        [
            shared_grad.reshape(tokens, groups, gu_cols).transpose(1, 0, 2),
            shared_hidden.reshape(tokens, groups, down_cols).transpose(1, 0, 2),
            jnp.zeros((groups, tokens, lanes - gu_cols - down_cols), jnp.bfloat16),
        ],
        axis=2,
    )
    back = lax.all_to_all(
        jnp.concatenate([shared_cols, low, high], axis=1),
        "expert",
        split_axis=0,
        concat_axis=0,
        tiled=True,
    )

    grad_down = dot(hidden, arrived, 0, 0).astype(jnp.bfloat16)
    grad_gate_up = dot(routed_inputs, routed_grad, 0, 0).astype(jnp.bfloat16)
    shared_back = dot(shared_grad, shared_gate_up, 1, 1)

    came_low = back[:, tokens : tokens + capacity].reshape(slots, lanes)
    came_high = back[:, tokens + capacity :].reshape(slots, lanes)
    came_back = jnp.concatenate([came_low, came_high[:, : width - lanes]], axis=1)
    grad_in = (shared_back + dot(sel, came_back, 0, 0)).astype(jnp.bfloat16)
    all_shared = back[:, :tokens].reshape(groups * tokens, lanes)
    shared_gu = dot(all_shared[:, :gu_cols], everyone[:, width : 2 * width], 0, 0)
    shared_dn = dot(all_shared[:, gu_cols : gu_cols + down_cols], everyone[:, :width], 0, 0)
    return (
        grad_in,
        grad_gate_up[None],
        grad_down[None],
        shared_gu.astype(jnp.bfloat16).T,
        shared_dn.astype(jnp.bfloat16),
    )


def solution(mesh):
    in_specs = (
        P("expert", "dp"),
        P("expert", None),
        P("expert", None),
        P("expert", "dp"),
        P("expert", None),
        P("expert", None, "dp"),
        P("expert", None, None),
        P("expert", "dp", None),
        P("expert", None, "dp"),
        P("dp", None),
        P(None, "dp"),
    )
    out_specs = (
        P("expert", "dp"),
        P("expert", "dp", None),
        P("expert", None, "dp"),
        P("dp", "expert"),
        P("expert", "dp"),
    )
    return jax.shard_map(
        on_device, mesh=mesh, in_specs=in_specs, out_specs=out_specs, check_vma=False
    )
```

```python
import jax
import jax.numpy as jnp
from jax import lax
from jax.experimental import pallas as pl
from jax.experimental.pallas import tpu as pltpu
from jax.sharding import PartitionSpec as P

NEAR = 4


LANES = 128
SLOT_ROWS = 16


def vmem(count):
    return [pl.BlockSpec(memory_space=pltpu.VMEM) for _ in range(count)]


def dot(a, b, ca, cb):
    return lax.dot_general(a, b, (((ca,), (cb,)), ((), ())), preferred_element_type=jnp.float32)


def route_kernel(capacity, ids_ref, gates_ref, grad_ref, sel_ref, out_ref):
    slots, tokens = sel_ref.shape
    slot = lax.broadcasted_iota(jnp.int32, (slots, 1), 0)
    expert = slot // SLOT_ROWS
    place = slot - expert * SLOT_ROWS
    place = jnp.where(place < capacity, place, tokens).astype(jnp.float32)
    ids = ids_ref[...]
    gates = gates_ref[...]
    hit = jnp.zeros((slots, tokens), jnp.float32)
    weight = jnp.zeros((slots, tokens), jnp.float32)
    for k in range(ids.shape[0]):
        same = ids[k : k + 1, :] == expert
        hit = jnp.where(same, 1.0, hit)
        weight = jnp.where(same, gates[k : k + 1, :], weight)
    row = lax.broadcasted_iota(jnp.int32, (tokens, tokens), 0)
    col = lax.broadcasted_iota(jnp.int32, (tokens, tokens), 1)
    earlier = jnp.where(row < col, 1.0, 0.0).astype(jnp.bfloat16)
    rank = jnp.dot(hit.astype(jnp.bfloat16), earlier, preferred_element_type=jnp.float32)
    taken = (hit > 0.0) & (rank == place)
    sel = jnp.where(taken, 1.0, 0.0).astype(jnp.bfloat16)
    gate = jnp.sum(jnp.where(taken, weight, 0.0), axis=1, keepdims=True)
    rows = jnp.dot(sel, grad_ref[...], preferred_element_type=jnp.float32)
    sel_ref[...] = sel
    scaled = (gate * rows).reshape(slots // SLOT_ROWS, SLOT_ROWS, rows.shape[1])
    out_ref[...] = scaled[:, :capacity, :].astype(jnp.bfloat16)


def swiglu_terms(gate, up, grad_hidden):
    sig = jax.nn.sigmoid(gate)
    act = gate * sig
    return grad_hidden * up * sig * (1.0 + gate * (1.0 - sig)), grad_hidden * act, act * up


def middle_kernel(
    capacity,
    full_ref,
    routed_pre_ref,
    shared_pre_ref,
    w_ref,
    shared_w_ref,
    grad_pre_ref,
    payload_ref,
    shared_back_ref,
):
    slots = routed_pre_ref.shape[0]
    tokens = shared_pre_ref.shape[0]
    half = full_ref.shape[1]
    width = w_ref.shape[0]
    groups = payload_ref.shape[0]
    step = 16
    for r in range(0, slots, step):
        for c in range(0, half, half // 2):
            part = half // 2
            d_gate, d_up, _ = swiglu_terms(
                routed_pre_ref[r : r + step, c : c + part].astype(jnp.float32),
                routed_pre_ref[r : r + step, half + c : half + c + part].astype(jnp.float32),
                full_ref[r : r + step, c : c + part].astype(jnp.float32),
            )
            grad_pre_ref[r : r + step, c : c + part] = d_gate.astype(jnp.bfloat16)
            grad_pre_ref[r : r + step, half + c : half + c + part] = d_up.astype(jnp.bfloat16)
    d_gate, d_up, value = swiglu_terms(
        shared_pre_ref[:, :half].astype(jnp.float32),
        shared_pre_ref[:, half:].astype(jnp.float32),
        full_ref[slots:, :].astype(jnp.float32),
    )
    d_gate, d_up = d_gate.astype(jnp.bfloat16), d_up.astype(jnp.bfloat16)
    value = value.astype(jnp.bfloat16)
    shared_back_ref[...] = dot(d_gate, shared_w_ref[:, :half], 1, 1) + dot(
        d_up, shared_w_ref[:, half:], 1, 1
    )
    gu_cols, down_cols = 2 * half // groups, half // groups
    for j in range(groups):
        source = d_gate if j < groups // 2 else d_up
        at = j % (groups // 2) * gu_cols
        payload_ref[j, :tokens, :gu_cols] = source[:, at : at + gu_cols]
        payload_ref[j, :tokens, gu_cols : gu_cols + down_cols] = value[
            :, j * down_cols : (j + 1) * down_cols
        ]
    used = gu_cols + down_cols
    payload_ref[:, :tokens, used:] = jnp.zeros((groups, tokens, LANES - used), jnp.bfloat16)
    returned = dot(grad_pre_ref[...], w_ref[...], 1, 1).astype(jnp.bfloat16)
    row = lax.broadcasted_iota(jnp.int32, (groups * SLOT_ROWS, slots), 0)
    col = lax.broadcasted_iota(jnp.int32, (groups * SLOT_ROWS, slots), 1)
    expert = row // SLOT_ROWS
    place = row - expert * SLOT_ROWS
    wanted = jnp.where(place < capacity, expert * capacity + place, -1)
    spread = jnp.where(wanted == col, 1.0, 0.0).astype(jnp.bfloat16)
    spaced = dot(spread, returned, 1, 0).astype(jnp.bfloat16)
    spaced = spaced.reshape(groups, SLOT_ROWS, width)
    payload_ref[:, tokens : tokens + SLOT_ROWS, :] = spaced[:, :, :LANES]
    payload_ref[:, tokens + SLOT_ROWS :, : width - LANES] = spaced[:, :, LANES:]
    payload_ref[:, tokens + SLOT_ROWS :, width - LANES :] = jnp.zeros(
        (groups, SLOT_ROWS, 2 * LANES - width), jnp.bfloat16
    )


def last_kernel(
    back_ref, sel_ref, shared_back_ref, everyone_ref, grad_in_ref, shared_gu_ref, shared_dn_ref
):
    groups = back_ref.shape[0]
    slots, tokens = sel_ref.shape
    gu_cols, width = shared_gu_ref.shape
    down_cols = shared_dn_ref.shape[0]
    low = back_ref[:, tokens : tokens + SLOT_ROWS, :].reshape(slots, LANES)
    high = back_ref[:, tokens + SLOT_ROWS :, :].reshape(slots, LANES)
    sel = sel_ref[...]
    shared_back = shared_back_ref[...]
    grad_in_ref[:, :LANES] = (shared_back[:, :LANES] + dot(sel, low, 0, 0)).astype(jnp.bfloat16)
    grad_in_ref[:, LANES:] = (
        shared_back[:, LANES:] + dot(sel, high, 0, 0)[:, : width - LANES]
    ).astype(jnp.bfloat16)
    shared = back_ref[:, :tokens, :].reshape(groups * tokens, LANES)
    grads = dot(shared, everyone_ref[...], 0, 0)
    shared_gu_ref[...] = grads[:gu_cols, 2 * LANES : 2 * LANES + width].astype(jnp.bfloat16)
    shared_dn_ref[...] = grads[gu_cols : gu_cols + down_cols, :width].astype(jnp.bfloat16)


def total(parts):
    acc = parts[0].astype(jnp.float32)
    for i in range(1, parts.shape[0]):
        acc = acc + parts[i].astype(jnp.float32)
    return acc.astype(jnp.bfloat16)


def on_device(
    grad_out,
    expert_ids,
    gate_weights,
    layer_inputs,
    shared_pre,
    routed_inputs,
    routed_pre,
    w_gate_up,
    w_down,
    shared_gate_up,
    shared_down,
):
    groups = lax.axis_size("expert")
    ring = lax.axis_size("dp")
    far = ring // NEAR
    near_groups = [[NEAR * a + b for b in range(NEAR)] for a in range(far)]
    far_groups = [[NEAR * a + b for a in range(far)] for b in range(NEAR)]
    slots = routed_pre.shape[1]
    capacity = slots // groups
    tokens, width = grad_out.shape
    hidden_width = w_down.shape[1]
    routed_pre, routed_inputs = routed_pre[0], routed_inputs[0]
    w_gate_up, w_down = w_gate_up[0], w_down[0]

    limit = pltpu.CompilerParams(vmem_limit_bytes=16 * 1024 * 1024)
    pad = jnp.zeros((tokens, 2 * LANES - width), jnp.bfloat16)
    everyone = lax.all_gather(
        jnp.concatenate([grad_out, pad, layer_inputs, pad], axis=1), "expert", axis=0, tiled=True
    )

    sel, outgoing = pl.pallas_call(
        lambda *refs: route_kernel(capacity, *refs),
        out_shape=(
            jax.ShapeDtypeStruct((groups * SLOT_ROWS, tokens), jnp.bfloat16),
            jax.ShapeDtypeStruct((groups, capacity, width), jnp.bfloat16),
        ),
        compiler_params=limit,
        name="route",
    )(expert_ids.T, gate_weights.T, grad_out)
    arrived = lax.all_to_all(
        outgoing, "expert", split_axis=0, concat_axis=0, tiled=True
    ).reshape(slots, width)

    part = jnp.concatenate(
        [dot(arrived, w_down, 1, 1), dot(grad_out, shared_down, 1, 1)], axis=0
    ).astype(jnp.bfloat16)
    rows = (slots + tokens) // NEAR
    cols = hidden_width // far
    near = lax.all_to_all(
        part.reshape(NEAR, rows, hidden_width),
        "dp",
        split_axis=0,
        concat_axis=0,
        tiled=True,
        axis_index_groups=near_groups,
    )
    near = total(near)
    near = near.reshape(rows, far, cols).transpose(1, 0, 2)
    distant = lax.all_to_all(
        near,
        "dp",
        split_axis=0,
        concat_axis=0,
        tiled=True,
        axis_index_groups=far_groups,
    )
    own = total(distant)
    full = lax.all_gather(own, "dp", axis=1, tiled=True, axis_index_groups=far_groups)
    full = lax.all_gather(full, "dp", axis=0, tiled=True, axis_index_groups=near_groups)

    grad_pre, payload, shared_back = pl.pallas_call(
        lambda *refs: middle_kernel(capacity, *refs),
        out_shape=(
            jax.ShapeDtypeStruct((slots, 2 * hidden_width), jnp.bfloat16),
            jax.ShapeDtypeStruct((groups, tokens + 2 * SLOT_ROWS, LANES), jnp.bfloat16),
            jax.ShapeDtypeStruct((tokens, width), jnp.float32),
        ),
        in_specs=vmem(5),
        out_specs=vmem(3),
        compiler_params=limit,
        name="middle",
    )(full, routed_pre, shared_pre, w_gate_up, shared_gate_up)
    back = lax.all_to_all(payload, "expert", split_axis=0, concat_axis=0, tiled=True)

    gate = routed_pre[:, :hidden_width].astype(jnp.float32)
    up = routed_pre[:, hidden_width:].astype(jnp.float32)
    hidden = (gate * jax.nn.sigmoid(gate) * up).astype(jnp.bfloat16)
    grad_down = dot(hidden, arrived, 0, 0).astype(jnp.bfloat16)
    grad_gate_up = dot(routed_inputs, grad_pre, 0, 0).astype(jnp.bfloat16)

    gu_cols = 2 * hidden_width // groups
    down_cols = hidden_width // groups
    grad_in, shared_gu, shared_dn = pl.pallas_call(
        last_kernel,
        out_shape=(
            jax.ShapeDtypeStruct((tokens, width), jnp.bfloat16),
            jax.ShapeDtypeStruct((gu_cols, width), jnp.bfloat16),
            jax.ShapeDtypeStruct((down_cols, width), jnp.bfloat16),
        ),
        in_specs=vmem(4),
        compiler_params=limit,
        name="last",
    )(back, sel, shared_back, everyone)
    return (
        grad_in,
        grad_gate_up[None],
        grad_down[None],
        shared_gu.T,
        shared_dn,
    )


def solution(mesh):
    in_specs = (
        P("expert", "dp"),
        P("expert", None),
        P("expert", None),
        P("expert", "dp"),
        P("expert", None),
        P("expert", None, "dp"),
        P("expert", None, None),
        P("expert", "dp", None),
        P("expert", None, "dp"),
        P("dp", None),
        P(None, "dp"),
    )
    out_specs = (
        P("expert", "dp"),
        P("expert", "dp", None),
        P("expert", None, "dp"),
        P("dp", "expert"),
        P("expert", "dp"),
    )
    return jax.shard_map(
        on_device, mesh=mesh, in_specs=in_specs, out_specs=out_specs, check_vma=False
    )
```

```python
import jax
import jax.numpy as jnp
from jax import lax
from jax.experimental import pallas as pl
from jax.experimental.pallas import tpu as pltpu
from jax.sharding import PartitionSpec as P

NEAR = 4


LANES = 128
SLOT_ROWS = 16


def in_hbm(x):
    return pltpu.with_memory_space_constraint(x, pltpu.HBM)


def vmem(count):
    return [pl.BlockSpec(memory_space=pltpu.VMEM) for _ in range(count)]


def dot(a, b, ca, cb):
    return lax.dot_general(a, b, (((ca,), (cb,)), ((), ())), preferred_element_type=jnp.float32)


def route_kernel(capacity, ids_hbm, gates_hbm, grad_hbm, sel_ref, out_ref, ids_ref, gates_ref, grad_ref, sems):
    copies = [
        pltpu.make_async_copy(source, target, sems.at[i])
        for i, (source, target) in enumerate(
            ((ids_hbm, ids_ref), (gates_hbm, gates_ref), (grad_hbm, grad_ref))
        )
    ]
    for copy in copies:
        copy.start()
    slots, tokens = sel_ref.shape
    slot = lax.broadcasted_iota(jnp.int32, (slots, 1), 0)
    expert = slot // SLOT_ROWS
    place = slot - expert * SLOT_ROWS
    place = jnp.where(place < capacity, place, tokens).astype(jnp.float32)
    for copy in copies:
        copy.wait()
    ids = ids_ref[...]
    gates = gates_ref[...]
    hit = jnp.zeros((slots, tokens), jnp.float32)
    weight = jnp.zeros((slots, tokens), jnp.float32)
    for k in range(ids.shape[0]):
        same = ids[k : k + 1, :] == expert
        hit = jnp.where(same, 1.0, hit)
        weight = jnp.where(same, gates[k : k + 1, :], weight)
    row = lax.broadcasted_iota(jnp.int32, (tokens, tokens), 0)
    col = lax.broadcasted_iota(jnp.int32, (tokens, tokens), 1)
    earlier = jnp.where(row < col, 1.0, 0.0).astype(jnp.bfloat16)
    rank = jnp.dot(hit.astype(jnp.bfloat16), earlier, preferred_element_type=jnp.float32)
    taken = (hit > 0.0) & (rank == place)
    sel = jnp.where(taken, 1.0, 0.0).astype(jnp.bfloat16)
    gate = jnp.sum(jnp.where(taken, weight, 0.0), axis=1, keepdims=True)
    rows = jnp.dot(sel, grad_ref[...], preferred_element_type=jnp.float32)
    sel_ref[...] = sel
    scaled = (gate * rows).reshape(slots // SLOT_ROWS, SLOT_ROWS, rows.shape[1])
    out_ref[...] = scaled[:, :capacity, :].astype(jnp.bfloat16)


def swiglu_terms(gate, up, grad_hidden):
    sig = jax.nn.sigmoid(gate)
    act = gate * sig
    return grad_hidden * up * sig * (1.0 + gate * (1.0 - sig)), grad_hidden * act, act * up


def middle_kernel(
    capacity,
    full_ref,
    routed_pre_ref,
    shared_pre_ref,
    w_ref,
    shared_w_hbm,
    grad_pre_hbm,
    payload_ref,
    shared_back_ref,
    shared_w_ref,
    grad_pre_ref,
    sems,
):
    shared_in = pltpu.make_async_copy(shared_w_hbm, shared_w_ref, sems.at[0])
    shared_in.start()
    slots = routed_pre_ref.shape[0]
    tokens = shared_pre_ref.shape[0]
    half = full_ref.shape[1]
    width = w_ref.shape[0]
    groups = payload_ref.shape[0]
    step = 16
    for r in range(0, slots, step):
        for c in range(0, half, half // 2):
            part = half // 2
            d_gate, d_up, _ = swiglu_terms(
                routed_pre_ref[r : r + step, c : c + part].astype(jnp.float32),
                routed_pre_ref[r : r + step, half + c : half + c + part].astype(jnp.float32),
                full_ref[r : r + step, c : c + part].astype(jnp.float32),
            )
            grad_pre_ref[r : r + step, c : c + part] = d_gate.astype(jnp.bfloat16)
            grad_pre_ref[r : r + step, half + c : half + c + part] = d_up.astype(jnp.bfloat16)
    grad_pre_out = pltpu.make_async_copy(grad_pre_ref, grad_pre_hbm, sems.at[1])
    grad_pre_out.start()
    d_gate, d_up, value = swiglu_terms(
        shared_pre_ref[:, :half].astype(jnp.float32),
        shared_pre_ref[:, half:].astype(jnp.float32),
        full_ref[slots:, :].astype(jnp.float32),
    )
    d_gate, d_up = d_gate.astype(jnp.bfloat16), d_up.astype(jnp.bfloat16)
    value = value.astype(jnp.bfloat16)
    shared_in.wait()
    shared_back_ref[...] = dot(d_gate, shared_w_ref[:, :half], 1, 1) + dot(
        d_up, shared_w_ref[:, half:], 1, 1
    )
    gu_cols, down_cols = 2 * half // groups, half // groups
    for j in range(groups):
        source = d_gate if j < groups // 2 else d_up
        at = j % (groups // 2) * gu_cols
        payload_ref[j, :tokens, :gu_cols] = source[:, at : at + gu_cols]
        payload_ref[j, :tokens, gu_cols : gu_cols + down_cols] = value[
            :, j * down_cols : (j + 1) * down_cols
        ]
    used = gu_cols + down_cols
    payload_ref[:, :tokens, used:] = jnp.zeros((groups, tokens, LANES - used), jnp.bfloat16)
    returned = dot(grad_pre_ref[...], w_ref[...], 1, 1).astype(jnp.bfloat16)
    row = lax.broadcasted_iota(jnp.int32, (groups * SLOT_ROWS, slots), 0)
    col = lax.broadcasted_iota(jnp.int32, (groups * SLOT_ROWS, slots), 1)
    expert = row // SLOT_ROWS
    place = row - expert * SLOT_ROWS
    wanted = jnp.where(place < capacity, expert * capacity + place, -1)
    spread = jnp.where(wanted == col, 1.0, 0.0).astype(jnp.bfloat16)
    spaced = dot(spread, returned, 1, 0).astype(jnp.bfloat16)
    spaced = spaced.reshape(groups, SLOT_ROWS, width)
    payload_ref[:, tokens : tokens + SLOT_ROWS, :] = spaced[:, :, :LANES]
    payload_ref[:, tokens + SLOT_ROWS :, : width - LANES] = spaced[:, :, LANES:]
    payload_ref[:, tokens + SLOT_ROWS :, width - LANES :] = jnp.zeros(
        (groups, SLOT_ROWS, 2 * LANES - width), jnp.bfloat16
    )
    grad_pre_out.wait()


def last_kernel(
    back_ref,
    sel_ref,
    shared_back_ref,
    everyone_hbm,
    grad_in_ref,
    shared_gu_ref,
    shared_dn_ref,
    everyone_ref,
    sem,
):
    everyone_in = pltpu.make_async_copy(everyone_hbm, everyone_ref, sem)
    everyone_in.start()
    groups = back_ref.shape[0]
    slots, tokens = sel_ref.shape
    gu_cols, width = shared_gu_ref.shape
    down_cols = shared_dn_ref.shape[0]
    low = back_ref[:, tokens : tokens + SLOT_ROWS, :].reshape(slots, LANES)
    high = back_ref[:, tokens + SLOT_ROWS :, :].reshape(slots, LANES)
    sel = sel_ref[...]
    shared_back = shared_back_ref[...]
    grad_in_ref[:, :LANES] = (shared_back[:, :LANES] + dot(sel, low, 0, 0)).astype(jnp.bfloat16)
    grad_in_ref[:, LANES:] = (
        shared_back[:, LANES:] + dot(sel, high, 0, 0)[:, : width - LANES]
    ).astype(jnp.bfloat16)
    shared = back_ref[:, :tokens, :].reshape(groups * tokens, LANES)
    everyone_in.wait()
    grads = dot(shared, everyone_ref[...], 0, 0)
    shared_gu_ref[...] = grads[:gu_cols, 2 * LANES : 2 * LANES + width].astype(jnp.bfloat16)
    shared_dn_ref[...] = grads[gu_cols : gu_cols + down_cols, :width].astype(jnp.bfloat16)


def total(parts):
    acc = parts[0].astype(jnp.float32)
    for i in range(1, parts.shape[0]):
        acc = acc + parts[i].astype(jnp.float32)
    return acc.astype(jnp.bfloat16)


def on_device(
    grad_out,
    expert_ids,
    gate_weights,
    layer_inputs,
    shared_pre,
    routed_inputs,
    routed_pre,
    w_gate_up,
    w_down,
    shared_gate_up,
    shared_down,
):
    groups = lax.axis_size("expert")
    ring = lax.axis_size("dp")
    far = ring // NEAR
    near_groups = [[NEAR * a + b for b in range(NEAR)] for a in range(far)]
    far_groups = [[NEAR * a + b for a in range(far)] for b in range(NEAR)]
    slots = routed_pre.shape[1]
    capacity = slots // groups
    tokens, width = grad_out.shape
    hidden_width = w_down.shape[1]
    routed_pre, routed_inputs = routed_pre[0], routed_inputs[0]
    w_gate_up, w_down = w_gate_up[0], w_down[0]

    limit = pltpu.CompilerParams(vmem_limit_bytes=16 * 1024 * 1024)
    pad = jnp.zeros((tokens, 2 * LANES - width), jnp.bfloat16)
    everyone = lax.all_gather(
        jnp.concatenate([grad_out, pad, layer_inputs, pad], axis=1), "expert", axis=0, tiled=True
    )

    sel, outgoing = pl.pallas_call(
        lambda *refs: route_kernel(capacity, *refs),
        out_shape=(
            jax.ShapeDtypeStruct((groups * SLOT_ROWS, tokens), jnp.bfloat16),
            jax.ShapeDtypeStruct((groups, capacity, width), jnp.bfloat16),
        ),
        in_specs=[pl.BlockSpec(memory_space=pltpu.HBM)] * 3,
        scratch_shapes=[
            pltpu.VMEM(expert_ids.shape[::-1], jnp.int32),
            pltpu.VMEM(gate_weights.shape[::-1], jnp.float32),
            pltpu.VMEM(grad_out.shape, jnp.bfloat16),
            pltpu.SemaphoreType.DMA((3,)),
        ],
        compiler_params=limit,
        name="route",
    )(*[in_hbm(x) for x in (expert_ids.T, gate_weights.T, grad_out)])
    arrived = lax.all_to_all(
        outgoing, "expert", split_axis=0, concat_axis=0, tiled=True
    ).reshape(slots, width)

    part = jnp.concatenate(
        [dot(arrived, w_down, 1, 1), dot(grad_out, shared_down, 1, 1)], axis=0
    ).astype(jnp.bfloat16)
    rows = (slots + tokens) // NEAR
    cols = hidden_width // far
    near = lax.all_to_all(
        part.reshape(NEAR, rows, hidden_width),
        "dp",
        split_axis=0,
        concat_axis=0,
        tiled=True,
        axis_index_groups=near_groups,
    )
    near = total(near)
    near = near.reshape(rows, far, cols).transpose(1, 0, 2)
    distant = lax.all_to_all(
        near,
        "dp",
        split_axis=0,
        concat_axis=0,
        tiled=True,
        axis_index_groups=far_groups,
    )
    own = total(distant)
    full = lax.all_gather(own, "dp", axis=1, tiled=True, axis_index_groups=far_groups)
    full = lax.all_gather(full, "dp", axis=0, tiled=True, axis_index_groups=near_groups)

    grad_pre, payload, shared_back = pl.pallas_call(
        lambda *refs: middle_kernel(capacity, *refs),
        out_shape=(
            pltpu.HBM((slots, 2 * hidden_width), jnp.bfloat16),
            jax.ShapeDtypeStruct((groups, tokens + 2 * SLOT_ROWS, LANES), jnp.bfloat16),
            jax.ShapeDtypeStruct((tokens, width), jnp.float32),
        ),
        in_specs=vmem(4) + [pl.BlockSpec(memory_space=pltpu.HBM)],
        out_specs=[pl.BlockSpec(memory_space=pltpu.HBM)] + vmem(2),
        scratch_shapes=[
            pltpu.VMEM(shared_gate_up.shape, jnp.bfloat16),
            pltpu.VMEM((slots, 2 * hidden_width), jnp.bfloat16),
            pltpu.SemaphoreType.DMA((2,)),
        ],
        compiler_params=limit,
        name="middle",
    )(full, routed_pre, shared_pre, w_gate_up, in_hbm(shared_gate_up))
    back = lax.all_to_all(payload, "expert", split_axis=0, concat_axis=0, tiled=True)

    gate = routed_pre[:, :hidden_width].astype(jnp.float32)
    up = routed_pre[:, hidden_width:].astype(jnp.float32)
    hidden = (gate * jax.nn.sigmoid(gate) * up).astype(jnp.bfloat16)
    grad_down = dot(hidden, arrived, 0, 0).astype(jnp.bfloat16)
    grad_gate_up = dot(routed_inputs, grad_pre, 0, 0).astype(jnp.bfloat16)

    gu_cols = 2 * hidden_width // groups
    down_cols = hidden_width // groups
    grad_in, shared_gu, shared_dn = pl.pallas_call(
        last_kernel,
        out_shape=(
            jax.ShapeDtypeStruct((tokens, width), jnp.bfloat16),
            jax.ShapeDtypeStruct((gu_cols, width), jnp.bfloat16),
            jax.ShapeDtypeStruct((down_cols, width), jnp.bfloat16),
        ),
        in_specs=vmem(3) + [pl.BlockSpec(memory_space=pltpu.HBM)],
        scratch_shapes=[pltpu.VMEM(everyone.shape, jnp.bfloat16), pltpu.SemaphoreType.DMA],
        compiler_params=limit,
        name="last",
    )(back, sel, shared_back, in_hbm(everyone))
    return (
        grad_in,
        grad_gate_up[None],
        grad_down[None],
        shared_gu.T,
        shared_dn,
    )


def solution(mesh):
    in_specs = (
        P("expert", "dp"),
        P("expert", None),
        P("expert", None),
        P("expert", "dp"),
        P("expert", None),
        P("expert", None, "dp"),
        P("expert", None, None),
        P("expert", "dp", None),
        P("expert", None, "dp"),
        P("dp", None),
        P(None, "dp"),
    )
    out_specs = (
        P("expert", "dp"),
        P("expert", "dp", None),
        P("expert", None, "dp"),
        P("dp", "expert"),
        P("expert", "dp"),
    )
    return jax.shard_map(
        on_device, mesh=mesh, in_specs=in_specs, out_specs=out_specs, check_vma=False
    )
```

```python
import jax
import jax.numpy as jnp
from jax import lax
from jax.experimental import pallas as pl
from jax.experimental.pallas import tpu as pltpu
from jax.sharding import PartitionSpec as P

NEAR = 4


LANES = 128
SLOT_ROWS = 16


def in_hbm(x):
    return pltpu.with_memory_space_constraint(x, pltpu.HBM)


def vmem(count):
    return [pl.BlockSpec(memory_space=pltpu.VMEM) for _ in range(count)]


def dot(a, b, ca, cb):
    return lax.dot_general(a, b, (((ca,), (cb,)), ((), ())), preferred_element_type=jnp.float32)


def route_kernel(
    capacity,
    ids_hbm,
    gates_hbm,
    grad_hbm,
    inputs_hbm,
    sel_ref,
    out_ref,
    ids_ref,
    gates_ref,
    grad_ref,
    inputs_ref,
    sems,
):
    copies = [
        pltpu.make_async_copy(source, target, sems.at[i])
        for i, (source, target) in enumerate(
            (
                (ids_hbm, ids_ref),
                (gates_hbm, gates_ref),
                (grad_hbm, grad_ref),
                (inputs_hbm, inputs_ref),
            )
        )
    ]
    for copy in copies:
        copy.start()
    slots, tokens = sel_ref.shape
    slot = lax.broadcasted_iota(jnp.int32, (slots, 1), 0)
    expert = slot // SLOT_ROWS
    place = slot - expert * SLOT_ROWS
    place = jnp.where(place < capacity, place, tokens).astype(jnp.float32)
    for copy in copies:
        copy.wait()
    ids = ids_ref[...]
    gates = gates_ref[...]
    hit = jnp.zeros((slots, tokens), jnp.float32)
    weight = jnp.zeros((slots, tokens), jnp.float32)
    for k in range(ids.shape[0]):
        same = ids[k : k + 1, :] == expert
        hit = jnp.where(same, 1.0, hit)
        weight = jnp.where(same, gates[k : k + 1, :], weight)
    row = lax.broadcasted_iota(jnp.int32, (tokens, tokens), 0)
    col = lax.broadcasted_iota(jnp.int32, (tokens, tokens), 1)
    earlier = jnp.where(row < col, 1.0, 0.0).astype(jnp.bfloat16)
    rank = jnp.dot(hit.astype(jnp.bfloat16), earlier, preferred_element_type=jnp.float32)
    taken = (hit > 0.0) & (rank == place)
    sel = jnp.where(taken, 1.0, 0.0).astype(jnp.bfloat16)
    gate = jnp.sum(jnp.where(taken, weight, 0.0), axis=1, keepdims=True)
    rows = jnp.dot(sel, grad_ref[...], preferred_element_type=jnp.float32)
    sel_ref[...] = sel
    scaled = (gate * rows).reshape(slots // SLOT_ROWS, SLOT_ROWS, rows.shape[1])
    out_ref[:, tokens:, :] = scaled[:, :capacity, :].astype(jnp.bfloat16)
    for j in range(out_ref.shape[0]):
        out_ref[j, :tokens, :] = grad_ref[...] if j % 2 else inputs_ref[...]


def swiglu_terms(gate, up, grad_hidden):
    sig = jax.nn.sigmoid(gate)
    act = gate * sig
    return grad_hidden * up * sig * (1.0 + gate * (1.0 - sig)), grad_hidden * act, act * up


def middle_kernel(
    capacity,
    full_ref,
    routed_pre_ref,
    shared_pre_ref,
    w_ref,
    shared_w_hbm,
    grad_pre_hbm,
    payload_ref,
    shared_back_ref,
    shared_w_ref,
    grad_pre_ref,
    sems,
):
    shared_in = pltpu.make_async_copy(shared_w_hbm, shared_w_ref, sems.at[0])
    shared_in.start()
    slots = routed_pre_ref.shape[0]
    tokens = shared_pre_ref.shape[0]
    half = full_ref.shape[1]
    width = w_ref.shape[0]
    groups = payload_ref.shape[0]
    step = 16
    for r in range(0, slots, step):
        for c in range(0, half, half // 2):
            part = half // 2
            d_gate, d_up, _ = swiglu_terms(
                routed_pre_ref[r : r + step, c : c + part].astype(jnp.float32),
                routed_pre_ref[r : r + step, half + c : half + c + part].astype(jnp.float32),
                full_ref[r : r + step, c : c + part].astype(jnp.float32),
            )
            grad_pre_ref[r : r + step, c : c + part] = d_gate.astype(jnp.bfloat16)
            grad_pre_ref[r : r + step, half + c : half + c + part] = d_up.astype(jnp.bfloat16)
    grad_pre_out = pltpu.make_async_copy(grad_pre_ref, grad_pre_hbm, sems.at[1])
    grad_pre_out.start()
    d_gate, d_up, value = swiglu_terms(
        shared_pre_ref[:, :half].astype(jnp.float32),
        shared_pre_ref[:, half:].astype(jnp.float32),
        full_ref[slots:, :].astype(jnp.float32),
    )
    d_gate, d_up = d_gate.astype(jnp.bfloat16), d_up.astype(jnp.bfloat16)
    value = value.astype(jnp.bfloat16)
    shared_in.wait()
    shared_back_ref[...] = dot(d_gate, shared_w_ref[:, :half], 1, 1) + dot(
        d_up, shared_w_ref[:, half:], 1, 1
    )
    gu_cols, down_cols = 2 * half // groups, half // groups
    for j in range(groups):
        source = d_gate if j < groups // 2 else d_up
        at = j % (groups // 2) * gu_cols
        payload_ref[j, :tokens, :gu_cols] = source[:, at : at + gu_cols]
        payload_ref[j, :tokens, gu_cols : gu_cols + down_cols] = value[
            :, j * down_cols : (j + 1) * down_cols
        ]
    used = gu_cols + down_cols
    payload_ref[:, :tokens, used:] = jnp.zeros((groups, tokens, LANES - used), jnp.bfloat16)
    returned = dot(grad_pre_ref[...], w_ref[...], 1, 1).astype(jnp.bfloat16)
    row = lax.broadcasted_iota(jnp.int32, (groups * SLOT_ROWS, slots), 0)
    col = lax.broadcasted_iota(jnp.int32, (groups * SLOT_ROWS, slots), 1)
    expert = row // SLOT_ROWS
    place = row - expert * SLOT_ROWS
    wanted = jnp.where(place < capacity, expert * capacity + place, -1)
    spread = jnp.where(wanted == col, 1.0, 0.0).astype(jnp.bfloat16)
    spaced = dot(spread, returned, 1, 0).astype(jnp.bfloat16)
    spaced = spaced.reshape(groups, SLOT_ROWS, width)
    payload_ref[:, tokens : tokens + SLOT_ROWS, :] = spaced[:, :, :LANES]
    payload_ref[:, tokens + SLOT_ROWS :, : width - LANES] = spaced[:, :, LANES:]
    payload_ref[:, tokens + SLOT_ROWS :, width - LANES :] = jnp.zeros(
        (groups, SLOT_ROWS, 2 * LANES - width), jnp.bfloat16
    )
    grad_pre_out.wait()


def last_kernel(
    parity_ref,
    back_ref,
    sel_ref,
    shared_back_ref,
    kept_hbm,
    other_hbm,
    grad_in_ref,
    shared_gu_ref,
    shared_dn_ref,
    inputs_ref,
    grads_ref,
    sems,
):
    odd = parity_ref[0] == 1

    @pl.when(odd)
    def _():
        pltpu.make_async_copy(other_hbm, inputs_ref, sems.at[0]).start()
        pltpu.make_async_copy(kept_hbm, grads_ref, sems.at[1]).start()

    @pl.when(jnp.logical_not(odd))
    def _():
        pltpu.make_async_copy(kept_hbm, inputs_ref, sems.at[0]).start()
        pltpu.make_async_copy(other_hbm, grads_ref, sems.at[1]).start()

    groups = back_ref.shape[0]
    slots, tokens = sel_ref.shape
    gu_cols, width = shared_gu_ref.shape
    down_cols = shared_dn_ref.shape[0]
    low = back_ref[:, tokens : tokens + SLOT_ROWS, :].reshape(slots, LANES)
    high = back_ref[:, tokens + SLOT_ROWS :, :].reshape(slots, LANES)
    sel = sel_ref[...]
    shared_back = shared_back_ref[...]
    grad_in_ref[:, :LANES] = (shared_back[:, :LANES] + dot(sel, low, 0, 0)).astype(jnp.bfloat16)
    grad_in_ref[:, LANES:] = (
        shared_back[:, LANES:] + dot(sel, high, 0, 0)[:, : width - LANES]
    ).astype(jnp.bfloat16)
    shared = back_ref[:, :tokens, :].reshape(groups * tokens, LANES)
    pltpu.make_async_copy(kept_hbm, inputs_ref, sems.at[0]).wait()
    pltpu.make_async_copy(other_hbm, grads_ref, sems.at[1]).wait()
    shared_gu_ref[...] = dot(shared, inputs_ref[...], 0, 0)[:gu_cols].astype(jnp.bfloat16)
    shared_dn_ref[...] = dot(shared, grads_ref[...], 0, 0)[gu_cols : gu_cols + down_cols].astype(
        jnp.bfloat16
    )


def total(parts):
    acc = parts[0].astype(jnp.float32)
    for i in range(1, parts.shape[0]):
        acc = acc + parts[i].astype(jnp.float32)
    return acc.astype(jnp.bfloat16)


def on_device(
    grad_out,
    expert_ids,
    gate_weights,
    layer_inputs,
    shared_pre,
    routed_inputs,
    routed_pre,
    w_gate_up,
    w_down,
    shared_gate_up,
    shared_down,
):
    groups = lax.axis_size("expert")
    ring = lax.axis_size("dp")
    far = ring // NEAR
    near_groups = [[NEAR * a + b for b in range(NEAR)] for a in range(far)]
    far_groups = [[NEAR * a + b for a in range(far)] for b in range(NEAR)]
    slots = routed_pre.shape[1]
    capacity = slots // groups
    tokens, width = grad_out.shape
    hidden_width = w_down.shape[1]
    routed_pre, routed_inputs = routed_pre[0], routed_inputs[0]
    w_gate_up, w_down = w_gate_up[0], w_down[0]

    limit = pltpu.CompilerParams(vmem_limit_bytes=16 * 1024 * 1024)
    sel, outgoing = pl.pallas_call(
        lambda *refs: route_kernel(capacity, *refs),
        out_shape=(
            jax.ShapeDtypeStruct((groups * SLOT_ROWS, tokens), jnp.bfloat16),
            jax.ShapeDtypeStruct((groups, tokens + capacity, width), jnp.bfloat16),
        ),
        in_specs=[pl.BlockSpec(memory_space=pltpu.HBM)] * 4,
        scratch_shapes=[
            pltpu.VMEM(expert_ids.shape[::-1], jnp.int32),
            pltpu.VMEM(gate_weights.shape[::-1], jnp.float32),
            pltpu.VMEM(grad_out.shape, jnp.bfloat16),
            pltpu.VMEM(layer_inputs.shape, jnp.bfloat16),
            pltpu.SemaphoreType.DMA((4,)),
        ],
        compiler_params=limit,
        name="route",
    )(*[in_hbm(x) for x in (expert_ids.T, gate_weights.T, grad_out, layer_inputs)])
    incoming = lax.all_to_all(outgoing, "expert", split_axis=0, concat_axis=0, tiled=True)
    arrived = incoming[:, tokens:].reshape(slots, width)
    kept = incoming[:, :tokens].reshape(groups * tokens, width)
    other = lax.ppermute(kept, "expert", [(i, i ^ 1) for i in range(groups)])
    parity = (lax.axis_index("expert") % 2).reshape(1).astype(jnp.int32)

    part = jnp.concatenate(
        [dot(arrived, w_down, 1, 1), dot(grad_out, shared_down, 1, 1)], axis=0
    ).astype(jnp.bfloat16)
    rows = (slots + tokens) // NEAR
    cols = hidden_width // far
    near = lax.all_to_all(
        part.reshape(NEAR, rows, hidden_width),
        "dp",
        split_axis=0,
        concat_axis=0,
        tiled=True,
        axis_index_groups=near_groups,
    )
    near = total(near)
    near = near.reshape(rows, far, cols).transpose(1, 0, 2)
    distant = lax.all_to_all(
        near,
        "dp",
        split_axis=0,
        concat_axis=0,
        tiled=True,
        axis_index_groups=far_groups,
    )
    own = total(distant)
    full = lax.all_gather(own, "dp", axis=1, tiled=True, axis_index_groups=far_groups)
    full = lax.all_gather(full, "dp", axis=0, tiled=True, axis_index_groups=near_groups)

    grad_pre, payload, shared_back = pl.pallas_call(
        lambda *refs: middle_kernel(capacity, *refs),
        out_shape=(
            pltpu.HBM((slots, 2 * hidden_width), jnp.bfloat16),
            jax.ShapeDtypeStruct((groups, tokens + 2 * SLOT_ROWS, LANES), jnp.bfloat16),
            jax.ShapeDtypeStruct((tokens, width), jnp.float32),
        ),
        in_specs=vmem(4) + [pl.BlockSpec(memory_space=pltpu.HBM)],
        out_specs=[pl.BlockSpec(memory_space=pltpu.HBM)] + vmem(2),
        scratch_shapes=[
            pltpu.VMEM(shared_gate_up.shape, jnp.bfloat16),
            pltpu.VMEM((slots, 2 * hidden_width), jnp.bfloat16),
            pltpu.SemaphoreType.DMA((2,)),
        ],
        compiler_params=limit,
        name="middle",
    )(full, routed_pre, shared_pre, w_gate_up, in_hbm(shared_gate_up))
    back = lax.all_to_all(payload, "expert", split_axis=0, concat_axis=0, tiled=True)

    gate = routed_pre[:, :hidden_width].astype(jnp.float32)
    up = routed_pre[:, hidden_width:].astype(jnp.float32)
    hidden = (gate * jax.nn.sigmoid(gate) * up).astype(jnp.bfloat16)
    grad_down = dot(hidden, arrived, 0, 0).astype(jnp.bfloat16)
    grad_gate_up = dot(routed_inputs, grad_pre, 0, 0).astype(jnp.bfloat16)

    gu_cols = 2 * hidden_width // groups
    down_cols = hidden_width // groups
    grad_in, shared_gu, shared_dn = pl.pallas_call(
        last_kernel,
        out_shape=(
            jax.ShapeDtypeStruct((tokens, width), jnp.bfloat16),
            jax.ShapeDtypeStruct((gu_cols, width), jnp.bfloat16),
            jax.ShapeDtypeStruct((down_cols, width), jnp.bfloat16),
        ),
        in_specs=[pl.BlockSpec(memory_space=pltpu.SMEM)]
        + vmem(3)
        + [pl.BlockSpec(memory_space=pltpu.HBM)] * 2,
        scratch_shapes=[
            pltpu.VMEM(kept.shape, jnp.bfloat16),
            pltpu.VMEM(kept.shape, jnp.bfloat16),
            pltpu.SemaphoreType.DMA((2,)),
        ],
        compiler_params=limit,
        name="last",
    )(parity, back, sel, shared_back, in_hbm(kept), in_hbm(other))
    return (
        grad_in,
        grad_gate_up[None],
        grad_down[None],
        shared_gu.T,
        shared_dn,
    )


def solution(mesh):
    in_specs = (
        P("expert", "dp"),
        P("expert", None),
        P("expert", None),
        P("expert", "dp"),
        P("expert", None),
        P("expert", None, "dp"),
        P("expert", None, None),
        P("expert", "dp", None),
        P("expert", None, "dp"),
        P("dp", None),
        P(None, "dp"),
    )
    out_specs = (
        P("expert", "dp"),
        P("expert", "dp", None),
        P("expert", None, "dp"),
        P("dp", "expert"),
        P("expert", "dp"),
    )
    return jax.shard_map(
        on_device, mesh=mesh, in_specs=in_specs, out_specs=out_specs, check_vma=False
    )
```

```python
import jax
import jax.numpy as jnp
from jax import lax
from jax.experimental import pallas as pl
from jax.experimental.pallas import tpu as pltpu
from jax.sharding import PartitionSpec as P

NEAR = 4


LANES = 128
SLOT_ROWS = 16


def in_hbm(x):
    return pltpu.with_memory_space_constraint(x, pltpu.HBM)


def vmem(count):
    return [pl.BlockSpec(memory_space=pltpu.VMEM) for _ in range(count)]


def dot(a, b, ca, cb):
    return lax.dot_general(a, b, (((ca,), (cb,)), ((), ())), preferred_element_type=jnp.float32)


def route_kernel(
    capacity,
    ids_hbm,
    gates_hbm,
    grad_hbm,
    inputs_hbm,
    sel_ref,
    out_ref,
    ids_ref,
    gates_ref,
    grad_ref,
    inputs_ref,
    sems,
):
    copies = [
        pltpu.make_async_copy(source, target, sems.at[i])
        for i, (source, target) in enumerate(
            (
                (ids_hbm, ids_ref),
                (gates_hbm, gates_ref),
                (grad_hbm, grad_ref),
                (inputs_hbm, inputs_ref),
            )
        )
    ]
    for copy in copies:
        copy.start()
    slots, tokens = sel_ref.shape
    slot = lax.broadcasted_iota(jnp.int32, (slots, 1), 0)
    expert = slot // SLOT_ROWS
    place = slot - expert * SLOT_ROWS
    place = jnp.where(place < capacity, place, tokens).astype(jnp.float32)
    for copy in copies:
        copy.wait()
    ids = ids_ref[...]
    gates = gates_ref[...]
    hit = jnp.zeros((slots, tokens), jnp.float32)
    weight = jnp.zeros((slots, tokens), jnp.float32)
    for k in range(ids.shape[0]):
        same = ids[k : k + 1, :] == expert
        hit = jnp.where(same, 1.0, hit)
        weight = jnp.where(same, gates[k : k + 1, :], weight)
    row = lax.broadcasted_iota(jnp.int32, (tokens, tokens), 0)
    col = lax.broadcasted_iota(jnp.int32, (tokens, tokens), 1)
    earlier = jnp.where(row < col, 1.0, 0.0).astype(jnp.bfloat16)
    rank = jnp.dot(hit.astype(jnp.bfloat16), earlier, preferred_element_type=jnp.float32)
    taken = (hit > 0.0) & (rank == place)
    sel = jnp.where(taken, 1.0, 0.0).astype(jnp.bfloat16)
    gate = jnp.sum(jnp.where(taken, weight, 0.0), axis=1, keepdims=True)
    rows = jnp.dot(sel, grad_ref[...], preferred_element_type=jnp.float32)
    sel_ref[...] = sel
    scaled = (gate * rows).reshape(slots // SLOT_ROWS, SLOT_ROWS, rows.shape[1])
    out_ref[:, tokens:, :] = scaled[:, :capacity, :].astype(jnp.bfloat16)
    for j in range(out_ref.shape[0]):
        out_ref[j, :tokens, :] = grad_ref[...] if j % 2 else inputs_ref[...]


def part_kernel(
    at_ref,
    arrived_ref,
    grad_ref,
    w_ref,
    shared_w_ref,
    own_ref,
    next_ref,
    last_ref,
    left_ref,
    right_ref,
    blocks_ref,
):
    rows, columns = own_ref.shape
    routed = dot(arrived_ref[...], w_ref[...], 1, 0)
    shared = dot(grad_ref[...], shared_w_ref[...], 1, 0)
    both = jnp.concatenate([routed, shared], axis=0)
    for b in range(NEAR):
        blocks_ref[b] = both[b * rows : (b + 1) * rows].astype(jnp.bfloat16)
    at = at_ref[0]
    own_ref[...] = blocks_ref[at]
    next_ref[...] = blocks_ref[lax.rem(at + 1, NEAR)]
    last_ref[...] = blocks_ref[lax.rem(at + NEAR - 1, NEAR)]
    opposite = lax.rem(at + 2, NEAR)
    left_ref[...] = blocks_ref[opposite, :, : columns // 2]
    right_ref[...] = blocks_ref[opposite, :, columns // 2 :]


def near_kernel(own_ref, after_ref, before_ref, ahead_ref, behind_ref, out_ref):
    far, _, cols = out_ref.shape
    f32 = jnp.float32
    for a in range(far):
        lanes = slice(a * cols, (a + 1) * cols)
        total = own_ref[:, lanes].astype(f32) + after_ref[:, lanes].astype(f32)
        total = total + before_ref[:, lanes].astype(f32)
        half = ahead_ref if a < far // 2 else behind_ref
        at = a % (far // 2) * cols
        out_ref[a] = (total + half[:, at : at + cols].astype(f32)).astype(jnp.bfloat16)


def swiglu_terms(gate, up, grad_hidden):
    sig = jax.nn.sigmoid(gate)
    act = gate * sig
    return grad_hidden * up * sig * (1.0 + gate * (1.0 - sig)), grad_hidden * act, act * up


def middle_kernel(
    capacity,
    full_ref,
    routed_pre_ref,
    shared_pre_ref,
    w_ref,
    shared_w_hbm,
    grad_pre_hbm,
    payload_ref,
    shared_back_ref,
    shared_w_ref,
    grad_pre_ref,
    sems,
):
    shared_in = pltpu.make_async_copy(shared_w_hbm, shared_w_ref, sems.at[0])
    shared_in.start()
    slots = routed_pre_ref.shape[0]
    tokens = shared_pre_ref.shape[0]
    half = full_ref.shape[1]
    width = w_ref.shape[0]
    groups = payload_ref.shape[0]
    step = 16
    for r in range(0, slots, step):
        for c in range(0, half, half // 2):
            part = half // 2
            d_gate, d_up, _ = swiglu_terms(
                routed_pre_ref[r : r + step, c : c + part].astype(jnp.float32),
                routed_pre_ref[r : r + step, half + c : half + c + part].astype(jnp.float32),
                full_ref[r : r + step, c : c + part].astype(jnp.float32),
            )
            grad_pre_ref[r : r + step, c : c + part] = d_gate.astype(jnp.bfloat16)
            grad_pre_ref[r : r + step, half + c : half + c + part] = d_up.astype(jnp.bfloat16)
    grad_pre_out = pltpu.make_async_copy(grad_pre_ref, grad_pre_hbm, sems.at[1])
    grad_pre_out.start()
    d_gate, d_up, value = swiglu_terms(
        shared_pre_ref[:, :half].astype(jnp.float32),
        shared_pre_ref[:, half:].astype(jnp.float32),
        full_ref[slots:, :].astype(jnp.float32),
    )
    d_gate, d_up = d_gate.astype(jnp.bfloat16), d_up.astype(jnp.bfloat16)
    value = value.astype(jnp.bfloat16)
    shared_in.wait()
    shared_back_ref[...] = dot(d_gate, shared_w_ref[:, :half], 1, 1) + dot(
        d_up, shared_w_ref[:, half:], 1, 1
    )
    gu_cols, down_cols = 2 * half // groups, half // groups
    for j in range(groups):
        source = d_gate if j < groups // 2 else d_up
        at = j % (groups // 2) * gu_cols
        payload_ref[j, :tokens, :gu_cols] = source[:, at : at + gu_cols]
        payload_ref[j, :tokens, gu_cols : gu_cols + down_cols] = value[
            :, j * down_cols : (j + 1) * down_cols
        ]
    used = gu_cols + down_cols
    payload_ref[:, :tokens, used:] = jnp.zeros((groups, tokens, LANES - used), jnp.bfloat16)
    returned = dot(grad_pre_ref[...], w_ref[...], 1, 1).astype(jnp.bfloat16)
    row = lax.broadcasted_iota(jnp.int32, (groups * SLOT_ROWS, slots), 0)
    col = lax.broadcasted_iota(jnp.int32, (groups * SLOT_ROWS, slots), 1)
    expert = row // SLOT_ROWS
    place = row - expert * SLOT_ROWS
    wanted = jnp.where(place < capacity, expert * capacity + place, -1)
    spread = jnp.where(wanted == col, 1.0, 0.0).astype(jnp.bfloat16)
    spaced = dot(spread, returned, 1, 0).astype(jnp.bfloat16)
    spaced = spaced.reshape(groups, SLOT_ROWS, width)
    payload_ref[:, tokens : tokens + SLOT_ROWS, :] = spaced[:, :, :LANES]
    payload_ref[:, tokens + SLOT_ROWS :, : width - LANES] = spaced[:, :, LANES:]
    payload_ref[:, tokens + SLOT_ROWS :, width - LANES :] = jnp.zeros(
        (groups, SLOT_ROWS, 2 * LANES - width), jnp.bfloat16
    )
    grad_pre_out.wait()


def last_kernel(
    parity_ref,
    back_ref,
    sel_ref,
    shared_back_ref,
    kept_hbm,
    other_hbm,
    grad_in_ref,
    shared_gu_ref,
    shared_dn_ref,
    inputs_ref,
    grads_ref,
    sems,
):
    odd = parity_ref[0] == 1

    @pl.when(odd)
    def _():
        pltpu.make_async_copy(other_hbm, inputs_ref, sems.at[0]).start()
        pltpu.make_async_copy(kept_hbm, grads_ref, sems.at[1]).start()

    @pl.when(jnp.logical_not(odd))
    def _():
        pltpu.make_async_copy(kept_hbm, inputs_ref, sems.at[0]).start()
        pltpu.make_async_copy(other_hbm, grads_ref, sems.at[1]).start()

    groups = back_ref.shape[0]
    slots, tokens = sel_ref.shape
    gu_cols, width = shared_gu_ref.shape
    down_cols = shared_dn_ref.shape[0]
    low = back_ref[:, tokens : tokens + SLOT_ROWS, :].reshape(slots, LANES)
    high = back_ref[:, tokens + SLOT_ROWS :, :].reshape(slots, LANES)
    sel = sel_ref[...]
    shared_back = shared_back_ref[...]
    grad_in_ref[:, :LANES] = (shared_back[:, :LANES] + dot(sel, low, 0, 0)).astype(jnp.bfloat16)
    grad_in_ref[:, LANES:] = (
        shared_back[:, LANES:] + dot(sel, high, 0, 0)[:, : width - LANES]
    ).astype(jnp.bfloat16)
    shared = back_ref[:, :tokens, :].reshape(groups * tokens, LANES)
    pltpu.make_async_copy(kept_hbm, inputs_ref, sems.at[0]).wait()
    pltpu.make_async_copy(other_hbm, grads_ref, sems.at[1]).wait()
    shared_gu_ref[...] = dot(shared, inputs_ref[...], 0, 0)[:gu_cols].astype(jnp.bfloat16)
    shared_dn_ref[...] = dot(shared, grads_ref[...], 0, 0)[gu_cols : gu_cols + down_cols].astype(
        jnp.bfloat16
    )


def total(parts):
    acc = parts[0].astype(jnp.float32)
    for i in range(1, parts.shape[0]):
        acc = acc + parts[i].astype(jnp.float32)
    return acc.astype(jnp.bfloat16)


def on_device(
    grad_out,
    expert_ids,
    gate_weights,
    layer_inputs,
    shared_pre,
    routed_inputs,
    routed_pre,
    w_gate_up,
    w_down,
    shared_gate_up,
    shared_down,
):
    groups = lax.axis_size("expert")
    ring = lax.axis_size("dp")
    far = ring // NEAR
    near_groups = [[NEAR * a + b for b in range(NEAR)] for a in range(far)]
    far_groups = [[NEAR * a + b for a in range(far)] for b in range(NEAR)]
    slots = routed_pre.shape[1]
    capacity = slots // groups
    tokens, width = grad_out.shape
    hidden_width = w_down.shape[1]
    routed_pre, routed_inputs = routed_pre[0], routed_inputs[0]
    w_gate_up, w_down = w_gate_up[0], w_down[0]

    limit = pltpu.CompilerParams(vmem_limit_bytes=16 * 1024 * 1024)
    sel, outgoing = pl.pallas_call(
        lambda *refs: route_kernel(capacity, *refs),
        out_shape=(
            jax.ShapeDtypeStruct((groups * SLOT_ROWS, tokens), jnp.bfloat16),
            jax.ShapeDtypeStruct((groups, tokens + capacity, width), jnp.bfloat16),
        ),
        in_specs=[pl.BlockSpec(memory_space=pltpu.HBM)] * 4,
        scratch_shapes=[
            pltpu.VMEM(expert_ids.shape[::-1], jnp.int32),
            pltpu.VMEM(gate_weights.shape[::-1], jnp.float32),
            pltpu.VMEM(grad_out.shape, jnp.bfloat16),
            pltpu.VMEM(layer_inputs.shape, jnp.bfloat16),
            pltpu.SemaphoreType.DMA((4,)),
        ],
        compiler_params=limit,
        name="route",
    )(*[in_hbm(x) for x in (expert_ids.T, gate_weights.T, grad_out, layer_inputs)])
    incoming = lax.all_to_all(outgoing, "expert", split_axis=0, concat_axis=0, tiled=True)
    arrived = incoming[:, tokens:].reshape(slots, width)
    kept = incoming[:, :tokens].reshape(groups * tokens, width)
    other = lax.ppermute(kept, "expert", [(i, i ^ 1) for i in range(groups)])
    parity = (lax.axis_index("expert") % 2).reshape(1).astype(jnp.int32)

    rows = (slots + tokens) // NEAR
    cols = hidden_width // far
    half = hidden_width // 2

    def shift(x, by):
        return lax.ppermute(x, "dp", [(i, (i + by) % ring) for i in range(ring)])

    def block(columns):
        return jax.ShapeDtypeStruct((rows, columns), jnp.bfloat16)

    quarter = (lax.axis_index("dp") % NEAR).reshape(1).astype(jnp.int32)
    own, to_next, to_last, to_right, to_left = pl.pallas_call(
        part_kernel,
        out_shape=(block(hidden_width),) * 3 + (block(half),) * 2,
        in_specs=[pl.BlockSpec(memory_space=pltpu.SMEM)] + vmem(4),
        out_specs=vmem(5),
        scratch_shapes=[pltpu.VMEM((NEAR, rows, hidden_width), jnp.bfloat16)],
        compiler_params=limit,
        name="part",
    )(quarter, arrived, grad_out, w_down.T, shared_down.T)
    near = pl.pallas_call(
        near_kernel,
        out_shape=jax.ShapeDtypeStruct((far, rows, cols), jnp.bfloat16),
        in_specs=vmem(5),
        out_specs=vmem(1)[0],
        compiler_params=limit,
        name="near",
    )(own, shift(to_next, 1), shift(to_last, -1), shift(to_right, 2), shift(to_left, -2))
    distant = lax.all_to_all(
        near,
        "dp",
        split_axis=0,
        concat_axis=0,
        tiled=True,
        axis_index_groups=far_groups,
    )
    own = total(distant)
    full = lax.all_gather(own, "dp", axis=1, tiled=True, axis_index_groups=far_groups)
    full = lax.all_gather(full, "dp", axis=0, tiled=True, axis_index_groups=near_groups)

    grad_pre, payload, shared_back = pl.pallas_call(
        lambda *refs: middle_kernel(capacity, *refs),
        out_shape=(
            pltpu.HBM((slots, 2 * hidden_width), jnp.bfloat16),
            jax.ShapeDtypeStruct((groups, tokens + 2 * SLOT_ROWS, LANES), jnp.bfloat16),
            jax.ShapeDtypeStruct((tokens, width), jnp.float32),
        ),
        in_specs=vmem(4) + [pl.BlockSpec(memory_space=pltpu.HBM)],
        out_specs=[pl.BlockSpec(memory_space=pltpu.HBM)] + vmem(2),
        scratch_shapes=[
            pltpu.VMEM(shared_gate_up.shape, jnp.bfloat16),
            pltpu.VMEM((slots, 2 * hidden_width), jnp.bfloat16),
            pltpu.SemaphoreType.DMA((2,)),
        ],
        compiler_params=limit,
        name="middle",
    )(full, routed_pre, shared_pre, w_gate_up, in_hbm(shared_gate_up))
    back = lax.all_to_all(payload, "expert", split_axis=0, concat_axis=0, tiled=True)

    gate = routed_pre[:, :hidden_width].astype(jnp.float32)
    up = routed_pre[:, hidden_width:].astype(jnp.float32)
    hidden = (gate * jax.nn.sigmoid(gate) * up).astype(jnp.bfloat16)
    grad_down = dot(hidden, arrived, 0, 0).astype(jnp.bfloat16)
    grad_gate_up = dot(routed_inputs, grad_pre, 0, 0).astype(jnp.bfloat16)

    gu_cols = 2 * hidden_width // groups
    down_cols = hidden_width // groups
    grad_in, shared_gu, shared_dn = pl.pallas_call(
        last_kernel,
        out_shape=(
            jax.ShapeDtypeStruct((tokens, width), jnp.bfloat16),
            jax.ShapeDtypeStruct((gu_cols, width), jnp.bfloat16),
            jax.ShapeDtypeStruct((down_cols, width), jnp.bfloat16),
        ),
        in_specs=[pl.BlockSpec(memory_space=pltpu.SMEM)]
        + vmem(3)
        + [pl.BlockSpec(memory_space=pltpu.HBM)] * 2,
        scratch_shapes=[
            pltpu.VMEM(kept.shape, jnp.bfloat16),
            pltpu.VMEM(kept.shape, jnp.bfloat16),
            pltpu.SemaphoreType.DMA((2,)),
        ],
        compiler_params=limit,
        name="last",
    )(parity, back, sel, shared_back, in_hbm(kept), in_hbm(other))
    return (
        grad_in,
        grad_gate_up[None],
        grad_down[None],
        shared_gu.T,
        shared_dn,
    )


def solution(mesh):
    in_specs = (
        P("expert", "dp"),
        P("expert", None),
        P("expert", None),
        P("expert", "dp"),
        P("expert", None),
        P("expert", None, "dp"),
        P("expert", None, None),
        P("expert", "dp", None),
        P("expert", None, "dp"),
        P("dp", None),
        P(None, "dp"),
    )
    out_specs = (
        P("expert", "dp"),
        P("expert", "dp", None),
        P("expert", None, "dp"),
        P("dp", "expert"),
        P("expert", "dp"),
    )
    return jax.shard_map(
        on_device, mesh=mesh, in_specs=in_specs, out_specs=out_specs, check_vma=False
    )
```

```python
import jax
import jax.numpy as jnp
from jax import lax
from jax.experimental import pallas as pl
from jax.experimental.pallas import tpu as pltpu
from jax.sharding import PartitionSpec as P

NEAR = 4


LANES = 128
SLOT_ROWS = 16


def in_hbm(x):
    return pltpu.with_memory_space_constraint(x, pltpu.HBM)


def vmem(count):
    return [pl.BlockSpec(memory_space=pltpu.VMEM) for _ in range(count)]


def dot(a, b, ca, cb):
    return lax.dot_general(a, b, (((ca,), (cb,)), ((), ())), preferred_element_type=jnp.float32)


def route_kernel(
    capacity,
    ids_hbm,
    gates_hbm,
    grad_hbm,
    inputs_hbm,
    sel_ref,
    out_ref,
    ids_ref,
    gates_ref,
    grad_ref,
    inputs_ref,
    sems,
):
    copies = [
        pltpu.make_async_copy(source, target, sems.at[i])
        for i, (source, target) in enumerate(
            (
                (ids_hbm, ids_ref),
                (gates_hbm, gates_ref),
                (grad_hbm, grad_ref),
                (inputs_hbm, inputs_ref),
            )
        )
    ]
    for copy in copies:
        copy.start()
    slots, tokens = sel_ref.shape
    slot = lax.broadcasted_iota(jnp.int32, (slots, 1), 0)
    expert = slot // SLOT_ROWS
    place = slot - expert * SLOT_ROWS
    place = jnp.where(place < capacity, place, tokens).astype(jnp.float32)
    for copy in copies:
        copy.wait()
    ids = ids_ref[...]
    gates = gates_ref[...]
    hit = jnp.zeros((slots, tokens), jnp.float32)
    weight = jnp.zeros((slots, tokens), jnp.float32)
    for k in range(ids.shape[0]):
        same = ids[k : k + 1, :] == expert
        hit = jnp.where(same, 1.0, hit)
        weight = jnp.where(same, gates[k : k + 1, :], weight)
    row = lax.broadcasted_iota(jnp.int32, (tokens, tokens), 0)
    col = lax.broadcasted_iota(jnp.int32, (tokens, tokens), 1)
    earlier = jnp.where(row < col, 1.0, 0.0).astype(jnp.bfloat16)
    rank = jnp.dot(hit.astype(jnp.bfloat16), earlier, preferred_element_type=jnp.float32)
    taken = (hit > 0.0) & (rank == place)
    sel = jnp.where(taken, 1.0, 0.0).astype(jnp.bfloat16)
    gate = jnp.sum(jnp.where(taken, weight, 0.0), axis=1, keepdims=True)
    rows = jnp.dot(sel, grad_ref[...], preferred_element_type=jnp.float32)
    sel_ref[...] = sel
    scaled = (gate * rows).reshape(slots // SLOT_ROWS, SLOT_ROWS, rows.shape[1])
    part = tokens // 2
    out_ref[:, part:, :] = scaled[:, :capacity, :].astype(jnp.bfloat16)
    for j in range(out_ref.shape[0]):
        source = grad_ref if j % 2 else inputs_ref
        at = j // 2 % 2 * part
        out_ref[j, :part, :] = source[at : at + part, :]


def part_kernel(
    at_ref,
    arrived_ref,
    grad_ref,
    w_ref,
    shared_w_ref,
    own_ref,
    next_ref,
    last_ref,
    left_ref,
    right_ref,
    blocks_ref,
):
    rows, columns = own_ref.shape
    routed = dot(arrived_ref[...], w_ref[...], 1, 0)
    shared = dot(grad_ref[...], shared_w_ref[...], 1, 0)
    both = jnp.concatenate([routed, shared], axis=0)
    for b in range(NEAR):
        blocks_ref[b] = both[b * rows : (b + 1) * rows].astype(jnp.bfloat16)
    at = at_ref[0]
    own_ref[...] = blocks_ref[at]
    next_ref[...] = blocks_ref[lax.rem(at + 1, NEAR)]
    last_ref[...] = blocks_ref[lax.rem(at + NEAR - 1, NEAR)]
    opposite = lax.rem(at + 2, NEAR)
    left_ref[...] = blocks_ref[opposite, :, : columns // 2]
    right_ref[...] = blocks_ref[opposite, :, columns // 2 :]


def near_kernel(own_ref, after_ref, before_ref, ahead_ref, behind_ref, out_ref):
    far, _, cols = out_ref.shape
    f32 = jnp.float32
    for a in range(far):
        lanes = slice(a * cols, (a + 1) * cols)
        total = own_ref[:, lanes].astype(f32) + after_ref[:, lanes].astype(f32)
        total = total + before_ref[:, lanes].astype(f32)
        half = ahead_ref if a < far // 2 else behind_ref
        at = a % (far // 2) * cols
        out_ref[a] = (total + half[:, at : at + cols].astype(f32)).astype(jnp.bfloat16)


def swiglu_terms(gate, up, grad_hidden):
    sig = jax.nn.sigmoid(gate)
    act = gate * sig
    return grad_hidden * up * sig * (1.0 + gate * (1.0 - sig)), grad_hidden * act, act * up


def middle_kernel(
    capacity,
    at_ref,
    own_ref,
    next_ref,
    last_ref,
    left_ref,
    right_ref,
    routed_pre_ref,
    shared_pre_ref,
    w_ref,
    shared_w_hbm,
    grad_pre_hbm,
    payload_ref,
    shared_back_ref,
    shared_w_ref,
    grad_pre_ref,
    full_ref,
    sems,
):
    shared_in = pltpu.make_async_copy(shared_w_hbm, shared_w_ref, sems.at[0])
    shared_in.start()
    rows, columns = own_ref.shape
    middle = columns // 2

    def place(turn, lanes, source_ref):
        row = pl.multiple_of(lax.rem(at_ref[0] + turn, NEAR) * rows, 8)
        full_ref[pl.ds(row, rows), lanes] = source_ref[...].astype(jnp.float32)

    place(0, slice(None), own_ref)
    place(1, slice(None), next_ref)
    place(NEAR - 1, slice(None), last_ref)
    place(2, slice(0, middle), left_ref)
    place(2, slice(middle, columns), right_ref)
    slots = routed_pre_ref.shape[0]
    tokens = shared_pre_ref.shape[0]
    half = full_ref.shape[1]
    width = w_ref.shape[0]
    groups = payload_ref.shape[0]
    step = 16
    for r in range(0, slots, step):
        for c in range(0, half, half // 2):
            part = half // 2
            d_gate, d_up, _ = swiglu_terms(
                routed_pre_ref[r : r + step, c : c + part].astype(jnp.float32),
                routed_pre_ref[r : r + step, half + c : half + c + part].astype(jnp.float32),
                full_ref[r : r + step, c : c + part],
            )
            grad_pre_ref[r : r + step, c : c + part] = d_gate.astype(jnp.bfloat16)
            grad_pre_ref[r : r + step, half + c : half + c + part] = d_up.astype(jnp.bfloat16)
    grad_pre_out = pltpu.make_async_copy(grad_pre_ref, grad_pre_hbm, sems.at[1])
    grad_pre_out.start()
    d_gate, d_up, value = swiglu_terms(
        shared_pre_ref[:, :half].astype(jnp.float32),
        shared_pre_ref[:, half:].astype(jnp.float32),
        full_ref[slots:, :],
    )
    d_gate, d_up = d_gate.astype(jnp.bfloat16), d_up.astype(jnp.bfloat16)
    value = value.astype(jnp.bfloat16)
    shared_in.wait()
    shared_back_ref[...] = dot(d_gate, shared_w_ref[:, :half], 1, 1) + dot(
        d_up, shared_w_ref[:, half:], 1, 1
    )
    gu_cols, down_cols = 2 * half // groups, half // groups
    for j in range(groups):
        source = d_gate if j < groups // 2 else d_up
        at = j % (groups // 2) * gu_cols
        payload_ref[j, :tokens, :gu_cols] = source[:, at : at + gu_cols]
        payload_ref[j, :tokens, gu_cols : gu_cols + down_cols] = value[
            :, j * down_cols : (j + 1) * down_cols
        ]
    used = gu_cols + down_cols
    payload_ref[:, :tokens, used:] = jnp.zeros((groups, tokens, LANES - used), jnp.bfloat16)
    returned = dot(grad_pre_ref[...], w_ref[...], 1, 1).astype(jnp.bfloat16)
    row = lax.broadcasted_iota(jnp.int32, (groups * SLOT_ROWS, slots), 0)
    col = lax.broadcasted_iota(jnp.int32, (groups * SLOT_ROWS, slots), 1)
    expert = row // SLOT_ROWS
    place = row - expert * SLOT_ROWS
    wanted = jnp.where(place < capacity, expert * capacity + place, -1)
    spread = jnp.where(wanted == col, 1.0, 0.0).astype(jnp.bfloat16)
    spaced = dot(spread, returned, 1, 0).astype(jnp.bfloat16)
    spaced = spaced.reshape(groups, SLOT_ROWS, width)
    payload_ref[:, tokens : tokens + SLOT_ROWS, :] = spaced[:, :, :LANES]
    payload_ref[:, tokens + SLOT_ROWS :, : width - LANES] = spaced[:, :, LANES:]
    payload_ref[:, tokens + SLOT_ROWS :, width - LANES :] = jnp.zeros(
        (groups, SLOT_ROWS, 2 * LANES - width), jnp.bfloat16
    )
    grad_pre_out.wait()


def last_kernel(
    order_ref,
    back_ref,
    sel_ref,
    shared_back_ref,
    first_hbm,
    second_hbm,
    third_hbm,
    fourth_hbm,
    grad_in_ref,
    shared_gu_ref,
    shared_dn_ref,
    pieces_ref,
    sems,
):
    copies = [
        pltpu.make_async_copy(source, pieces_ref.at[i], sems.at[i])
        for i, source in enumerate((first_hbm, second_hbm, third_hbm, fourth_hbm))
    ]
    for copy in copies:
        copy.start()
    groups = back_ref.shape[0]
    slots, tokens = sel_ref.shape
    gu_cols, width = shared_gu_ref.shape
    down_cols = shared_dn_ref.shape[0]
    low = back_ref[:, tokens : tokens + SLOT_ROWS, :].reshape(slots, LANES)
    high = back_ref[:, tokens + SLOT_ROWS :, :].reshape(slots, LANES)
    sel = sel_ref[...]
    shared_back = shared_back_ref[...]
    grad_in_ref[:, :LANES] = (shared_back[:, :LANES] + dot(sel, low, 0, 0)).astype(jnp.bfloat16)
    grad_in_ref[:, LANES:] = (
        shared_back[:, LANES:] + dot(sel, high, 0, 0)[:, : width - LANES]
    ).astype(jnp.bfloat16)
    for copy in copies:
        copy.wait()
    part = tokens // 2
    shared_gu = jnp.zeros((LANES, width), jnp.float32)
    shared_dn = jnp.zeros((LANES, width), jnp.float32)
    for h in range(2):
        shared = back_ref[:, h * part : (h + 1) * part, :].reshape(groups * part, LANES)
        inputs = pieces_ref[order_ref[2 * h]].reshape(groups * part, width)
        grads = pieces_ref[order_ref[2 * h + 1]].reshape(groups * part, width)
        shared_gu = shared_gu + dot(shared, inputs, 0, 0)
        shared_dn = shared_dn + dot(shared, grads, 0, 0)
    shared_gu_ref[...] = shared_gu[:gu_cols].astype(jnp.bfloat16)
    shared_dn_ref[...] = shared_dn[gu_cols : gu_cols + down_cols].astype(jnp.bfloat16)


def total(parts):
    acc = parts[0].astype(jnp.float32)
    for i in range(1, parts.shape[0]):
        acc = acc + parts[i].astype(jnp.float32)
    return acc.astype(jnp.bfloat16)


def on_device(
    grad_out,
    expert_ids,
    gate_weights,
    layer_inputs,
    shared_pre,
    routed_inputs,
    routed_pre,
    w_gate_up,
    w_down,
    shared_gate_up,
    shared_down,
):
    groups = lax.axis_size("expert")
    ring = lax.axis_size("dp")
    far = ring // NEAR
    far_groups = [[NEAR * a + b for a in range(far)] for b in range(NEAR)]
    slots = routed_pre.shape[1]
    capacity = slots // groups
    tokens, width = grad_out.shape
    hidden_width = w_down.shape[1]
    routed_pre, routed_inputs = routed_pre[0], routed_inputs[0]
    w_gate_up, w_down = w_gate_up[0], w_down[0]

    limit = pltpu.CompilerParams(vmem_limit_bytes=16 * 1024 * 1024)
    sel, outgoing = pl.pallas_call(
        lambda *refs: route_kernel(capacity, *refs),
        out_shape=(
            jax.ShapeDtypeStruct((groups * SLOT_ROWS, tokens), jnp.bfloat16),
            jax.ShapeDtypeStruct((groups, tokens // 2 + capacity, width), jnp.bfloat16),
        ),
        in_specs=[pl.BlockSpec(memory_space=pltpu.HBM)] * 4,
        scratch_shapes=[
            pltpu.VMEM(expert_ids.shape[::-1], jnp.int32),
            pltpu.VMEM(gate_weights.shape[::-1], jnp.float32),
            pltpu.VMEM(grad_out.shape, jnp.bfloat16),
            pltpu.VMEM(layer_inputs.shape, jnp.bfloat16),
            pltpu.SemaphoreType.DMA((4,)),
        ],
        compiler_params=limit,
        name="route",
    )(*[in_hbm(x) for x in (expert_ids.T, gate_weights.T, grad_out, layer_inputs)])
    incoming = lax.all_to_all(outgoing, "expert", split_axis=0, concat_axis=0, tiled=True)
    arrived = incoming[:, tokens // 2 :].reshape(slots, width)
    order = (lax.axis_index("expert") % 4).astype(jnp.int32) ^ jnp.arange(4, dtype=jnp.int32)

    rows = (slots + tokens) // NEAR
    cols = hidden_width // far
    half = hidden_width // 2

    def shift(x, by):
        return lax.ppermute(x, "dp", [(i, (i + by) % ring) for i in range(ring)])

    def block(columns):
        return jax.ShapeDtypeStruct((rows, columns), jnp.bfloat16)

    quarter = (lax.axis_index("dp") % NEAR).reshape(1).astype(jnp.int32)
    own, to_next, to_last, to_right, to_left = pl.pallas_call(
        part_kernel,
        out_shape=(block(hidden_width),) * 3 + (block(half),) * 2,
        in_specs=[pl.BlockSpec(memory_space=pltpu.SMEM)] + vmem(4),
        out_specs=vmem(5),
        scratch_shapes=[pltpu.VMEM((NEAR, rows, hidden_width), jnp.bfloat16)],
        compiler_params=limit,
        name="part",
    )(quarter, arrived, grad_out, w_down.T, shared_down.T)
    near = pl.pallas_call(
        near_kernel,
        out_shape=jax.ShapeDtypeStruct((far, rows, cols), jnp.bfloat16),
        in_specs=vmem(5),
        out_specs=vmem(1)[0],
        compiler_params=limit,
        name="near",
    )(own, shift(to_next, 1), shift(to_last, -1), shift(to_right, 2), shift(to_left, -2))
    near, piece = lax.optimization_barrier((near, incoming[:, : tokens // 2]))
    pieces = [piece]
    for turn in (1, 2, 3):
        pieces.append(lax.ppermute(piece, "expert", [(i, i ^ turn) for i in range(groups)]))
    distant = lax.all_to_all(
        near,
        "dp",
        split_axis=0,
        concat_axis=0,
        tiled=True,
        axis_index_groups=far_groups,
    )
    own, *pieces = lax.optimization_barrier((total(distant), *pieces))
    full = lax.all_gather(own, "dp", axis=1, tiled=True, axis_index_groups=far_groups)
    around = (
        shift(full, -1),
        shift(full, 1),
        shift(full[:, :half], 2),
        shift(full[:, half:], -2),
    )

    grad_pre, payload, shared_back = pl.pallas_call(
        lambda *refs: middle_kernel(capacity, *refs),
        out_shape=(
            pltpu.HBM((slots, 2 * hidden_width), jnp.bfloat16),
            jax.ShapeDtypeStruct((groups, tokens + 2 * SLOT_ROWS, LANES), jnp.bfloat16),
            jax.ShapeDtypeStruct((tokens, width), jnp.float32),
        ),
        in_specs=[pl.BlockSpec(memory_space=pltpu.SMEM)]
        + vmem(8)
        + [pl.BlockSpec(memory_space=pltpu.HBM)],
        out_specs=[pl.BlockSpec(memory_space=pltpu.HBM)] + vmem(2),
        scratch_shapes=[
            pltpu.VMEM(shared_gate_up.shape, jnp.bfloat16),
            pltpu.VMEM((slots, 2 * hidden_width), jnp.bfloat16),
            pltpu.VMEM((slots + tokens, hidden_width), jnp.float32),
            pltpu.SemaphoreType.DMA((2,)),
        ],
        compiler_params=limit,
        name="middle",
    )(quarter, full, *around, routed_pre, shared_pre, w_gate_up, in_hbm(shared_gate_up))
    back = lax.all_to_all(payload, "expert", split_axis=0, concat_axis=0, tiled=True)

    gate = routed_pre[:, :hidden_width].astype(jnp.float32)
    up = routed_pre[:, hidden_width:].astype(jnp.float32)
    hidden = (gate * jax.nn.sigmoid(gate) * up).astype(jnp.bfloat16)
    grad_down = dot(hidden, arrived, 0, 0).astype(jnp.bfloat16)
    grad_gate_up = dot(routed_inputs, grad_pre, 0, 0).astype(jnp.bfloat16)

    gu_cols = 2 * hidden_width // groups
    down_cols = hidden_width // groups
    grad_in, shared_gu, shared_dn = pl.pallas_call(
        last_kernel,
        out_shape=(
            jax.ShapeDtypeStruct((tokens, width), jnp.bfloat16),
            jax.ShapeDtypeStruct((gu_cols, width), jnp.bfloat16),
            jax.ShapeDtypeStruct((down_cols, width), jnp.bfloat16),
        ),
        in_specs=[pl.BlockSpec(memory_space=pltpu.SMEM)]
        + vmem(3)
        + [pl.BlockSpec(memory_space=pltpu.HBM)] * 4,
        scratch_shapes=[
            pltpu.VMEM((4, *pieces[0].shape), jnp.bfloat16),
            pltpu.SemaphoreType.DMA((4,)),
        ],
        compiler_params=limit,
        name="last",
    )(order, back, sel, shared_back, *[in_hbm(piece) for piece in pieces])
    return (
        grad_in,
        grad_gate_up[None],
        grad_down[None],
        shared_gu.T,
        shared_dn,
    )


def solution(mesh):
    in_specs = (
        P("expert", "dp"),
        P("expert", None),
        P("expert", None),
        P("expert", "dp"),
        P("expert", None),
        P("expert", None, "dp"),
        P("expert", None, None),
        P("expert", "dp", None),
        P("expert", None, "dp"),
        P("dp", None),
        P(None, "dp"),
    )
    out_specs = (
        P("expert", "dp"),
        P("expert", "dp", None),
        P("expert", None, "dp"),
        P("dp", "expert"),
        P("expert", "dp"),
    )
    return jax.shard_map(
        on_device, mesh=mesh, in_specs=in_specs, out_specs=out_specs, check_vma=False
    )
```

```python
import jax
import jax.numpy as jnp
from jax import lax
from jax.experimental import pallas as pl
from jax.experimental.pallas import tpu as pltpu
from jax.sharding import PartitionSpec as P

NEAR = 4


LANES = 128
SLOT_ROWS = 16


def in_hbm(x):
    return pltpu.with_memory_space_constraint(x, pltpu.HBM)


def vmem(count):
    return [pl.BlockSpec(memory_space=pltpu.VMEM) for _ in range(count)]


def dot(a, b, ca, cb):
    return lax.dot_general(a, b, (((ca,), (cb,)), ((), ())), preferred_element_type=jnp.float32)


def route_kernel(
    capacity,
    ids_hbm,
    gates_hbm,
    grad_hbm,
    inputs_hbm,
    sel_ref,
    out_ref,
    ids_ref,
    gates_ref,
    grad_ref,
    inputs_ref,
    sems,
):
    copies = [
        pltpu.make_async_copy(source, target, sems.at[i])
        for i, (source, target) in enumerate(
            (
                (ids_hbm, ids_ref),
                (gates_hbm, gates_ref),
                (grad_hbm, grad_ref),
                (inputs_hbm, inputs_ref),
            )
        )
    ]
    for copy in copies:
        copy.start()
    slots, tokens = sel_ref.shape
    slot = lax.broadcasted_iota(jnp.int32, (slots, 1), 0)
    expert = slot // SLOT_ROWS
    place = slot - expert * SLOT_ROWS
    place = jnp.where(place < capacity, place, tokens).astype(jnp.float32)
    for copy in copies:
        copy.wait()
    ids = ids_ref[...]
    gates = gates_ref[...]
    hit = jnp.zeros((slots, tokens), jnp.float32)
    weight = jnp.zeros((slots, tokens), jnp.float32)
    for k in range(ids.shape[0]):
        same = ids[k : k + 1, :] == expert
        hit = jnp.where(same, 1.0, hit)
        weight = jnp.where(same, gates[k : k + 1, :], weight)
    row = lax.broadcasted_iota(jnp.int32, (tokens, tokens), 0)
    col = lax.broadcasted_iota(jnp.int32, (tokens, tokens), 1)
    earlier = jnp.where(row < col, 1.0, 0.0).astype(jnp.bfloat16)
    rank = jnp.dot(hit.astype(jnp.bfloat16), earlier, preferred_element_type=jnp.float32)
    taken = (hit > 0.0) & (rank == place)
    sel = jnp.where(taken, 1.0, 0.0).astype(jnp.bfloat16)
    gate = jnp.sum(jnp.where(taken, weight, 0.0), axis=1, keepdims=True)
    rows = jnp.dot(sel, grad_ref[...], preferred_element_type=jnp.float32)
    sel_ref[...] = sel
    scaled = (gate * rows).reshape(slots // SLOT_ROWS, SLOT_ROWS, rows.shape[1])
    part = tokens // 2
    out_ref[:, part:, :] = scaled[:, :capacity, :].astype(jnp.bfloat16)
    for j in range(out_ref.shape[0]):
        source = grad_ref if j % 2 else inputs_ref
        at = j // 2 % 2 * part
        out_ref[j, :part, :] = source[at : at + part, :]


def part_kernel(
    at_ref,
    arrived_ref,
    grad_ref,
    w_ref,
    shared_w_ref,
    own_ref,
    next_ref,
    last_ref,
    left_ref,
    right_ref,
    blocks_ref,
):
    rows, columns = own_ref.shape
    routed = dot(arrived_ref[...], w_ref[...], 1, 0)
    shared = dot(grad_ref[...], shared_w_ref[...], 1, 0)
    both = jnp.concatenate([routed, shared], axis=0)
    for b in range(NEAR):
        blocks_ref[b] = both[b * rows : (b + 1) * rows].astype(jnp.bfloat16)
    at = at_ref[0]
    own_ref[...] = blocks_ref[at]
    next_ref[...] = blocks_ref[lax.rem(at + 1, NEAR)]
    last_ref[...] = blocks_ref[lax.rem(at + NEAR - 1, NEAR)]
    opposite = lax.rem(at + 2, NEAR)
    left_ref[...] = blocks_ref[opposite, :, : columns // 2]
    right_ref[...] = blocks_ref[opposite, :, columns // 2 :]


def near_kernel(own_ref, after_ref, before_ref, ahead_ref, behind_ref, out_ref):
    far, _, cols = out_ref.shape
    f32 = jnp.float32
    for a in range(far):
        lanes = slice(a * cols, (a + 1) * cols)
        total = own_ref[:, lanes].astype(f32) + after_ref[:, lanes].astype(f32)
        total = total + before_ref[:, lanes].astype(f32)
        half = ahead_ref if a < far // 2 else behind_ref
        at = a % (far // 2) * cols
        out_ref[a] = (total + half[:, at : at + cols].astype(f32)).astype(jnp.bfloat16)


def swiglu_terms(gate, up, grad_hidden):
    sig = jax.nn.sigmoid(gate)
    act = gate * sig
    return grad_hidden * up * sig * (1.0 + gate * (1.0 - sig)), grad_hidden * act, act * up


def middle_kernel(
    capacity,
    full_ref,
    routed_pre_ref,
    shared_pre_ref,
    w_ref,
    shared_w_hbm,
    grad_pre_hbm,
    payload_ref,
    shared_back_ref,
    shared_w_ref,
    grad_pre_ref,
    sems,
):
    shared_in = pltpu.make_async_copy(shared_w_hbm, shared_w_ref, sems.at[0])
    shared_in.start()
    slots = routed_pre_ref.shape[0]
    tokens = shared_pre_ref.shape[0]
    half = full_ref.shape[1]
    width = w_ref.shape[0]
    groups = payload_ref.shape[0]
    step = 16
    for r in range(0, slots, step):
        for c in range(0, half, half // 2):
            part = half // 2
            d_gate, d_up, _ = swiglu_terms(
                routed_pre_ref[r : r + step, c : c + part].astype(jnp.float32),
                routed_pre_ref[r : r + step, half + c : half + c + part].astype(jnp.float32),
                full_ref[r : r + step, c : c + part].astype(jnp.float32),
            )
            grad_pre_ref[r : r + step, c : c + part] = d_gate.astype(jnp.bfloat16)
            grad_pre_ref[r : r + step, half + c : half + c + part] = d_up.astype(jnp.bfloat16)
    grad_pre_out = pltpu.make_async_copy(grad_pre_ref, grad_pre_hbm, sems.at[1])
    grad_pre_out.start()
    d_gate, d_up, value = swiglu_terms(
        shared_pre_ref[:, :half].astype(jnp.float32),
        shared_pre_ref[:, half:].astype(jnp.float32),
        full_ref[slots:, :].astype(jnp.float32),
    )
    d_gate, d_up = d_gate.astype(jnp.bfloat16), d_up.astype(jnp.bfloat16)
    value = value.astype(jnp.bfloat16)
    shared_in.wait()
    shared_back_ref[...] = dot(d_gate, shared_w_ref[:, :half], 1, 1) + dot(
        d_up, shared_w_ref[:, half:], 1, 1
    )
    gu_cols, down_cols = 2 * half // groups, half // groups
    for j in range(groups):
        source = d_gate if j < groups // 2 else d_up
        at = j % (groups // 2) * gu_cols
        payload_ref[j, :tokens, :gu_cols] = source[:, at : at + gu_cols]
        payload_ref[j, :tokens, gu_cols : gu_cols + down_cols] = value[
            :, j * down_cols : (j + 1) * down_cols
        ]
    used = gu_cols + down_cols
    payload_ref[:, :tokens, used:] = jnp.zeros((groups, tokens, LANES - used), jnp.bfloat16)
    returned = dot(grad_pre_ref[...], w_ref[...], 1, 1).astype(jnp.bfloat16)
    row = lax.broadcasted_iota(jnp.int32, (groups * SLOT_ROWS, slots), 0)
    col = lax.broadcasted_iota(jnp.int32, (groups * SLOT_ROWS, slots), 1)
    expert = row // SLOT_ROWS
    place = row - expert * SLOT_ROWS
    wanted = jnp.where(place < capacity, expert * capacity + place, -1)
    spread = jnp.where(wanted == col, 1.0, 0.0).astype(jnp.bfloat16)
    spaced = dot(spread, returned, 1, 0).astype(jnp.bfloat16)
    spaced = spaced.reshape(groups, SLOT_ROWS, width)
    payload_ref[:, tokens : tokens + SLOT_ROWS, :] = spaced[:, :, :LANES]
    payload_ref[:, tokens + SLOT_ROWS :, : width - LANES] = spaced[:, :, LANES:]
    payload_ref[:, tokens + SLOT_ROWS :, width - LANES :] = jnp.zeros(
        (groups, SLOT_ROWS, 2 * LANES - width), jnp.bfloat16
    )
    grad_pre_out.wait()


def last_kernel(
    order_ref,
    back_ref,
    sel_ref,
    shared_back_ref,
    first_hbm,
    second_hbm,
    third_hbm,
    fourth_hbm,
    grad_in_ref,
    shared_gu_ref,
    shared_dn_ref,
    pieces_ref,
    sems,
):
    copies = [
        pltpu.make_async_copy(source, pieces_ref.at[i], sems.at[i])
        for i, source in enumerate((first_hbm, second_hbm, third_hbm, fourth_hbm))
    ]
    for copy in copies:
        copy.start()
    groups = back_ref.shape[0]
    slots, tokens = sel_ref.shape
    gu_cols, width = shared_gu_ref.shape
    down_cols = shared_dn_ref.shape[0]
    low = back_ref[:, tokens : tokens + SLOT_ROWS, :].reshape(slots, LANES)
    high = back_ref[:, tokens + SLOT_ROWS :, :].reshape(slots, LANES)
    sel = sel_ref[...]
    shared_back = shared_back_ref[...]
    grad_in_ref[:, :LANES] = (shared_back[:, :LANES] + dot(sel, low, 0, 0)).astype(jnp.bfloat16)
    grad_in_ref[:, LANES:] = (
        shared_back[:, LANES:] + dot(sel, high, 0, 0)[:, : width - LANES]
    ).astype(jnp.bfloat16)
    for copy in copies:
        copy.wait()
    part = tokens // 2
    shared_gu = jnp.zeros((LANES, width), jnp.float32)
    shared_dn = jnp.zeros((LANES, width), jnp.float32)
    for h in range(2):
        shared = back_ref[:, h * part : (h + 1) * part, :].reshape(groups * part, LANES).T
        inputs = pieces_ref[order_ref[2 * h]].reshape(groups * part, width)
        grads = pieces_ref[order_ref[2 * h + 1]].reshape(groups * part, width)
        shared_gu = shared_gu + dot(shared, inputs, 1, 0)
        shared_dn = shared_dn + dot(shared, grads, 1, 0)
    shared_gu_ref[...] = shared_gu[:gu_cols].astype(jnp.bfloat16)
    shared_dn_ref[...] = shared_dn[gu_cols : gu_cols + down_cols].astype(jnp.bfloat16)


def total(parts):
    acc = parts[0].astype(jnp.float32)
    for i in range(1, parts.shape[0]):
        acc = acc + parts[i].astype(jnp.float32)
    return acc.astype(jnp.bfloat16)


def on_device(
    grad_out,
    expert_ids,
    gate_weights,
    layer_inputs,
    shared_pre,
    routed_inputs,
    routed_pre,
    w_gate_up,
    w_down,
    shared_gate_up,
    shared_down,
):
    groups = lax.axis_size("expert")
    ring = lax.axis_size("dp")
    far = ring // NEAR
    near_groups = [[NEAR * a + b for b in range(NEAR)] for a in range(far)]
    far_groups = [[NEAR * a + b for a in range(far)] for b in range(NEAR)]
    slots = routed_pre.shape[1]
    capacity = slots // groups
    tokens, width = grad_out.shape
    hidden_width = w_down.shape[1]
    routed_pre, routed_inputs = routed_pre[0], routed_inputs[0]
    w_gate_up, w_down = w_gate_up[0], w_down[0]

    limit = pltpu.CompilerParams(vmem_limit_bytes=16 * 1024 * 1024)
    sel, outgoing = pl.pallas_call(
        lambda *refs: route_kernel(capacity, *refs),
        out_shape=(
            jax.ShapeDtypeStruct((groups * SLOT_ROWS, tokens), jnp.bfloat16),
            jax.ShapeDtypeStruct((groups, tokens // 2 + capacity, width), jnp.bfloat16),
        ),
        in_specs=[pl.BlockSpec(memory_space=pltpu.HBM)] * 4,
        scratch_shapes=[
            pltpu.VMEM(expert_ids.shape[::-1], jnp.int32),
            pltpu.VMEM(gate_weights.shape[::-1], jnp.float32),
            pltpu.VMEM(grad_out.shape, jnp.bfloat16),
            pltpu.VMEM(layer_inputs.shape, jnp.bfloat16),
            pltpu.SemaphoreType.DMA((4,)),
        ],
        compiler_params=limit,
        name="route",
    )(*[in_hbm(x) for x in (expert_ids.T, gate_weights.T, grad_out, layer_inputs)])
    incoming = lax.all_to_all(outgoing, "expert", split_axis=0, concat_axis=0, tiled=True)
    arrived = incoming[:, tokens // 2 :].reshape(slots, width)
    order = (lax.axis_index("expert") % 4).astype(jnp.int32) ^ jnp.arange(4, dtype=jnp.int32)

    rows = (slots + tokens) // NEAR
    cols = hidden_width // far
    half = hidden_width // 2

    def shift(x, by):
        return lax.ppermute(x, "dp", [(i, (i + by) % ring) for i in range(ring)])

    def block(columns):
        return jax.ShapeDtypeStruct((rows, columns), jnp.bfloat16)

    quarter = (lax.axis_index("dp") % NEAR).reshape(1).astype(jnp.int32)
    own, to_next, to_last, to_right, to_left = pl.pallas_call(
        part_kernel,
        out_shape=(block(hidden_width),) * 3 + (block(half),) * 2,
        in_specs=[pl.BlockSpec(memory_space=pltpu.SMEM)] + vmem(4),
        out_specs=vmem(5),
        scratch_shapes=[pltpu.VMEM((NEAR, rows, hidden_width), jnp.bfloat16)],
        compiler_params=limit,
        name="part",
    )(quarter, arrived, grad_out, w_down.T, shared_down.T)
    near = pl.pallas_call(
        near_kernel,
        out_shape=jax.ShapeDtypeStruct((far, rows, cols), jnp.bfloat16),
        in_specs=vmem(5),
        out_specs=vmem(1)[0],
        compiler_params=limit,
        name="near",
    )(own, shift(to_next, 1), shift(to_last, -1), shift(to_right, 2), shift(to_left, -2))
    near, piece = lax.optimization_barrier((near, incoming[:, : tokens // 2]))
    pieces = [piece]
    for turn in (1, 2, 3):
        pieces.append(lax.ppermute(piece, "expert", [(i, i ^ turn) for i in range(groups)]))
    distant = lax.all_to_all(
        near,
        "dp",
        split_axis=0,
        concat_axis=0,
        tiled=True,
        axis_index_groups=far_groups,
    )
    own = total(distant)
    full = lax.all_gather(own, "dp", axis=1, tiled=True, axis_index_groups=far_groups)
    full = lax.all_gather(full, "dp", axis=0, tiled=True, axis_index_groups=near_groups)

    grad_pre, payload, shared_back = pl.pallas_call(
        lambda *refs: middle_kernel(capacity, *refs),
        out_shape=(
            pltpu.HBM((slots, 2 * hidden_width), jnp.bfloat16),
            jax.ShapeDtypeStruct((groups, tokens + 2 * SLOT_ROWS, LANES), jnp.bfloat16),
            jax.ShapeDtypeStruct((tokens, width), jnp.float32),
        ),
        in_specs=vmem(4) + [pl.BlockSpec(memory_space=pltpu.HBM)],
        out_specs=[pl.BlockSpec(memory_space=pltpu.HBM)] + vmem(2),
        scratch_shapes=[
            pltpu.VMEM(shared_gate_up.shape, jnp.bfloat16),
            pltpu.VMEM((slots, 2 * hidden_width), jnp.bfloat16),
            pltpu.SemaphoreType.DMA((2,)),
        ],
        compiler_params=limit,
        name="middle",
    )(full, routed_pre, shared_pre, w_gate_up, in_hbm(shared_gate_up))
    back = lax.all_to_all(payload, "expert", split_axis=0, concat_axis=0, tiled=True)

    gate = routed_pre[:, :hidden_width].astype(jnp.float32)
    up = routed_pre[:, hidden_width:].astype(jnp.float32)
    hidden = (gate * jax.nn.sigmoid(gate) * up).astype(jnp.bfloat16)
    grad_down = dot(hidden, arrived, 0, 0).astype(jnp.bfloat16)
    grad_gate_up = dot(routed_inputs, grad_pre, 0, 0).astype(jnp.bfloat16)

    gu_cols = 2 * hidden_width // groups
    down_cols = hidden_width // groups
    grad_in, shared_gu, shared_dn = pl.pallas_call(
        last_kernel,
        out_shape=(
            jax.ShapeDtypeStruct((tokens, width), jnp.bfloat16),
            jax.ShapeDtypeStruct((gu_cols, width), jnp.bfloat16),
            jax.ShapeDtypeStruct((down_cols, width), jnp.bfloat16),
        ),
        in_specs=[pl.BlockSpec(memory_space=pltpu.SMEM)]
        + vmem(3)
        + [pl.BlockSpec(memory_space=pltpu.HBM)] * 4,
        scratch_shapes=[
            pltpu.VMEM((4, *pieces[0].shape), jnp.bfloat16),
            pltpu.SemaphoreType.DMA((4,)),
        ],
        compiler_params=limit,
        name="last",
    )(order, back, sel, shared_back, *[in_hbm(piece) for piece in pieces])
    return (
        grad_in,
        grad_gate_up[None],
        grad_down[None],
        shared_gu.T,
        shared_dn,
    )


def solution(mesh):
    in_specs = (
        P("expert", "dp"),
        P("expert", None),
        P("expert", None),
        P("expert", "dp"),
        P("expert", None),
        P("expert", None, "dp"),
        P("expert", None, None),
        P("expert", "dp", None),
        P("expert", None, "dp"),
        P("dp", None),
        P(None, "dp"),
    )
    out_specs = (
        P("expert", "dp"),
        P("expert", "dp", None),
        P("expert", None, "dp"),
        P("dp", "expert"),
        P("expert", "dp"),
    )
    return jax.shard_map(
        on_device, mesh=mesh, in_specs=in_specs, out_specs=out_specs, check_vma=False
    )
```

```python
import jax
import jax.numpy as jnp
from jax import lax
from jax.experimental import pallas as pl
from jax.experimental.pallas import tpu as pltpu
from jax.sharding import PartitionSpec as P

NEAR = 4


LANES = 128
SLOT_ROWS = 16


def in_hbm(x):
    return pltpu.with_memory_space_constraint(x, pltpu.HBM)


def vmem(count):
    return [pl.BlockSpec(memory_space=pltpu.VMEM) for _ in range(count)]


def dot(a, b, ca, cb):
    return lax.dot_general(a, b, (((ca,), (cb,)), ((), ())), preferred_element_type=jnp.float32)


def route_kernel(
    capacity,
    ids_hbm,
    gates_hbm,
    grad_hbm,
    inputs_hbm,
    sel_ref,
    out_ref,
    ids_ref,
    gates_ref,
    grad_ref,
    inputs_ref,
    sems,
):
    copies = [
        pltpu.make_async_copy(source, target, sems.at[i])
        for i, (source, target) in enumerate(
            (
                (ids_hbm, ids_ref),
                (gates_hbm, gates_ref),
                (grad_hbm, grad_ref),
                (inputs_hbm, inputs_ref),
            )
        )
    ]
    for copy in copies:
        copy.start()
    slots, tokens = sel_ref.shape
    slot = lax.broadcasted_iota(jnp.int32, (slots, 1), 0)
    expert = slot // SLOT_ROWS
    place = slot - expert * SLOT_ROWS
    place = jnp.where(place < capacity, place, tokens).astype(jnp.float32)
    for copy in copies:
        copy.wait()
    ids = ids_ref[...]
    gates = gates_ref[...]
    hit = jnp.zeros((slots, tokens), jnp.float32)
    weight = jnp.zeros((slots, tokens), jnp.float32)
    for k in range(ids.shape[0]):
        same = ids[k : k + 1, :] == expert
        hit = jnp.where(same, 1.0, hit)
        weight = jnp.where(same, gates[k : k + 1, :], weight)
    row = lax.broadcasted_iota(jnp.int32, (tokens, tokens), 0)
    col = lax.broadcasted_iota(jnp.int32, (tokens, tokens), 1)
    earlier = jnp.where(row < col, 1.0, 0.0).astype(jnp.bfloat16)
    rank = jnp.dot(hit.astype(jnp.bfloat16), earlier, preferred_element_type=jnp.float32)
    taken = (hit > 0.0) & (rank == place)
    sel = jnp.where(taken, 1.0, 0.0).astype(jnp.bfloat16)
    gate = jnp.sum(jnp.where(taken, weight, 0.0), axis=1, keepdims=True)
    rows = jnp.dot(sel, grad_ref[...], preferred_element_type=jnp.float32)
    sel_ref[...] = sel
    scaled = (gate * rows).reshape(slots // SLOT_ROWS, SLOT_ROWS, rows.shape[1])
    part = tokens // 2
    out_ref[:, part:, :] = scaled[:, :capacity, :].astype(jnp.bfloat16)
    for j in range(out_ref.shape[0]):
        source = grad_ref if j % 2 else inputs_ref
        at = j // 2 % 2 * part
        out_ref[j, :part, :] = source[at : at + part, :]


def part_kernel(
    at_ref,
    arrived_ref,
    grad_ref,
    w_ref,
    shared_w_ref,
    own_ref,
    next_ref,
    last_ref,
    left_ref,
    right_ref,
    blocks_ref,
):
    rows, columns = own_ref.shape
    routed = dot(arrived_ref[...], w_ref[...], 1, 0)
    shared = dot(grad_ref[...], shared_w_ref[...], 1, 0)
    both = jnp.concatenate([routed, shared], axis=0)
    for b in range(NEAR):
        blocks_ref[b] = both[b * rows : (b + 1) * rows].astype(jnp.bfloat16)
    at = at_ref[0]
    own_ref[...] = blocks_ref[at]
    next_ref[...] = blocks_ref[lax.rem(at + 1, NEAR)]
    last_ref[...] = blocks_ref[lax.rem(at + NEAR - 1, NEAR)]
    opposite = lax.rem(at + 2, NEAR)
    left_ref[...] = blocks_ref[opposite, :, : columns // 2]
    right_ref[...] = blocks_ref[opposite, :, columns // 2 :]


def near_kernel(own_ref, after_ref, before_ref, ahead_ref, behind_ref, out_ref):
    far, _, cols = out_ref.shape
    f32 = jnp.float32
    for a in range(far):
        lanes = slice(a * cols, (a + 1) * cols)
        total = own_ref[:, lanes].astype(f32) + after_ref[:, lanes].astype(f32)
        total = total + before_ref[:, lanes].astype(f32)
        half = ahead_ref if a < far // 2 else behind_ref
        at = a % (far // 2) * cols
        out_ref[a] = (total + half[:, at : at + cols].astype(f32)).astype(jnp.bfloat16)


def swiglu_terms(gate, up, grad_hidden):
    sig = jax.nn.sigmoid(gate)
    act = gate * sig
    return grad_hidden * up * sig * (1.0 + gate * (1.0 - sig)), grad_hidden * act, act * up


def middle_kernel(
    capacity,
    full_ref,
    routed_pre_ref,
    shared_pre_ref,
    w_ref,
    shared_w_hbm,
    grad_pre_hbm,
    payload_ref,
    shared_back_ref,
    shared_w_ref,
    grad_pre_ref,
    sems,
):
    shared_in = pltpu.make_async_copy(shared_w_hbm, shared_w_ref, sems.at[0])
    shared_in.start()
    slots = routed_pre_ref.shape[0]
    tokens = shared_pre_ref.shape[0]
    half = full_ref.shape[1]
    width = w_ref.shape[0]
    groups = payload_ref.shape[0]
    step = 16
    for r in range(0, slots, step):
        for c in range(0, half, half // 2):
            part = half // 2
            d_gate, d_up, _ = swiglu_terms(
                routed_pre_ref[r : r + step, c : c + part].astype(jnp.float32),
                routed_pre_ref[r : r + step, half + c : half + c + part].astype(jnp.float32),
                full_ref[r : r + step, c : c + part].astype(jnp.float32),
            )
            grad_pre_ref[r : r + step, c : c + part] = d_gate.astype(jnp.bfloat16)
            grad_pre_ref[r : r + step, half + c : half + c + part] = d_up.astype(jnp.bfloat16)
    grad_pre_out = pltpu.make_async_copy(grad_pre_ref, grad_pre_hbm, sems.at[1])
    grad_pre_out.start()
    d_gate, d_up, value = swiglu_terms(
        shared_pre_ref[:, :half].astype(jnp.float32),
        shared_pre_ref[:, half:].astype(jnp.float32),
        full_ref[slots:, :].astype(jnp.float32),
    )
    d_gate, d_up = d_gate.astype(jnp.bfloat16), d_up.astype(jnp.bfloat16)
    value = value.astype(jnp.bfloat16)
    shared_in.wait()
    shared_back_ref[...] = dot(d_gate, shared_w_ref[:, :half], 1, 1) + dot(
        d_up, shared_w_ref[:, half:], 1, 1
    )
    gu_cols, down_cols = 2 * half // groups, half // groups
    for j in range(groups):
        source = d_gate if j < groups // 2 else d_up
        at = j % (groups // 2) * gu_cols
        payload_ref[j, :tokens, :gu_cols] = source[:, at : at + gu_cols]
        payload_ref[j, :tokens, gu_cols : gu_cols + down_cols] = value[
            :, j * down_cols : (j + 1) * down_cols
        ]
    used = gu_cols + down_cols
    payload_ref[:, :tokens, used:] = jnp.zeros((groups, tokens, LANES - used), jnp.bfloat16)
    returned = dot(grad_pre_ref[...], w_ref[...], 1, 1).astype(jnp.bfloat16)
    row = lax.broadcasted_iota(jnp.int32, (groups * SLOT_ROWS, slots), 0)
    col = lax.broadcasted_iota(jnp.int32, (groups * SLOT_ROWS, slots), 1)
    expert = row // SLOT_ROWS
    place = row - expert * SLOT_ROWS
    wanted = jnp.where(place < capacity, expert * capacity + place, -1)
    spread = jnp.where(wanted == col, 1.0, 0.0).astype(jnp.bfloat16)
    spaced = dot(spread, returned, 1, 0).astype(jnp.bfloat16)
    spaced = spaced.reshape(groups, SLOT_ROWS, width)
    payload_ref[:, tokens : tokens + SLOT_ROWS, :] = spaced[:, :, :LANES]
    payload_ref[:, tokens + SLOT_ROWS :, : width - LANES] = spaced[:, :, LANES:]
    payload_ref[:, tokens + SLOT_ROWS :, width - LANES :] = jnp.zeros(
        (groups, SLOT_ROWS, 2 * LANES - width), jnp.bfloat16
    )
    grad_pre_out.wait()


def last_kernel(
    turn_ref,
    back_ref,
    sel_ref,
    shared_back_ref,
    first_hbm,
    second_hbm,
    third_hbm,
    fourth_hbm,
    grad_in_ref,
    shared_gu_ref,
    shared_dn_ref,
    pieces_ref,
    sems,
):
    copies = [
        pltpu.make_async_copy(source, pieces_ref.at[i], sems.at[i])
        for i, source in enumerate((first_hbm, second_hbm, third_hbm, fourth_hbm))
    ]
    for copy in copies:
        copy.start()
    groups = back_ref.shape[0]
    slots, tokens = sel_ref.shape
    gu_cols, width = shared_gu_ref.shape
    down_cols = shared_dn_ref.shape[0]
    low = back_ref[:, tokens : tokens + SLOT_ROWS, :].reshape(slots, LANES)
    high = back_ref[:, tokens + SLOT_ROWS :, :].reshape(slots, LANES)
    sel = sel_ref[...]
    shared_back = shared_back_ref[...]
    grad_in_ref[:, :LANES] = (shared_back[:, :LANES] + dot(sel, low, 0, 0)).astype(jnp.bfloat16)
    grad_in_ref[:, LANES:] = (
        shared_back[:, LANES:] + dot(sel, high, 0, 0)[:, : width - LANES]
    ).astype(jnp.bfloat16)
    for copy in copies:
        copy.wait()
    part = tokens // 2
    shared_gu = jnp.zeros((LANES, width), jnp.float32)
    shared_dn = jnp.zeros((LANES, width), jnp.float32)
    for h in range(2):
        shared = back_ref[:, h * part : (h + 1) * part, :].reshape(groups * part, LANES).T
        inputs = pieces_ref[jnp.bitwise_xor(turn_ref[0], 2 * h)].reshape(groups * part, width)
        grads = pieces_ref[jnp.bitwise_xor(turn_ref[0], 2 * h + 1)].reshape(groups * part, width)
        shared_gu = shared_gu + dot(shared, inputs, 1, 0)
        shared_dn = shared_dn + dot(shared, grads, 1, 0)
    shared_gu_ref[...] = shared_gu[:gu_cols].astype(jnp.bfloat16)
    shared_dn_ref[...] = shared_dn[gu_cols : gu_cols + down_cols].astype(jnp.bfloat16)


def total(parts):
    acc = parts[0].astype(jnp.float32)
    for i in range(1, parts.shape[0]):
        acc = acc + parts[i].astype(jnp.float32)
    return acc.astype(jnp.bfloat16)


def on_device(
    grad_out,
    expert_ids,
    gate_weights,
    layer_inputs,
    shared_pre,
    routed_inputs,
    routed_pre,
    w_gate_up,
    w_down,
    shared_gate_up,
    shared_down,
):
    groups = lax.axis_size("expert")
    ring = lax.axis_size("dp")
    far = ring // NEAR
    near_groups = [[NEAR * a + b for b in range(NEAR)] for a in range(far)]
    far_groups = [[NEAR * a + b for a in range(far)] for b in range(NEAR)]
    slots = routed_pre.shape[1]
    capacity = slots // groups
    tokens, width = grad_out.shape
    hidden_width = w_down.shape[1]
    routed_pre, routed_inputs = routed_pre[0], routed_inputs[0]
    w_gate_up, w_down = w_gate_up[0], w_down[0]

    limit = pltpu.CompilerParams(vmem_limit_bytes=16 * 1024 * 1024)
    sel, outgoing = pl.pallas_call(
        lambda *refs: route_kernel(capacity, *refs),
        out_shape=(
            jax.ShapeDtypeStruct((groups * SLOT_ROWS, tokens), jnp.bfloat16),
            jax.ShapeDtypeStruct((groups, tokens // 2 + capacity, width), jnp.bfloat16),
        ),
        in_specs=[pl.BlockSpec(memory_space=pltpu.HBM)] * 4,
        scratch_shapes=[
            pltpu.VMEM(expert_ids.shape[::-1], jnp.int32),
            pltpu.VMEM(gate_weights.shape[::-1], jnp.float32),
            pltpu.VMEM(grad_out.shape, jnp.bfloat16),
            pltpu.VMEM(layer_inputs.shape, jnp.bfloat16),
            pltpu.SemaphoreType.DMA((4,)),
        ],
        compiler_params=limit,
        name="route",
    )(*[in_hbm(x) for x in (expert_ids.T, gate_weights.T, grad_out, layer_inputs)])
    incoming = lax.all_to_all(outgoing, "expert", split_axis=0, concat_axis=0, tiled=True)
    arrived = incoming[:, tokens // 2 :].reshape(slots, width)
    turn_of = (lax.axis_index("expert") % 4).reshape(1).astype(jnp.int32)

    rows = (slots + tokens) // NEAR
    cols = hidden_width // far
    half = hidden_width // 2

    def shift(x, by):
        return lax.ppermute(x, "dp", [(i, (i + by) % ring) for i in range(ring)])

    def block(columns):
        return jax.ShapeDtypeStruct((rows, columns), jnp.bfloat16)

    quarter = (lax.axis_index("dp") % NEAR).reshape(1).astype(jnp.int32)
    own, to_next, to_last, to_right, to_left = pl.pallas_call(
        part_kernel,
        out_shape=(block(hidden_width),) * 3 + (block(half),) * 2,
        in_specs=[pl.BlockSpec(memory_space=pltpu.SMEM)] + vmem(4),
        out_specs=vmem(5),
        scratch_shapes=[pltpu.VMEM((NEAR, rows, hidden_width), jnp.bfloat16)],
        compiler_params=limit,
        name="part",
    )(quarter, arrived, grad_out, w_down.T, shared_down.T)
    near = pl.pallas_call(
        near_kernel,
        out_shape=jax.ShapeDtypeStruct((far, rows, cols), jnp.bfloat16),
        in_specs=vmem(5),
        out_specs=vmem(1)[0],
        compiler_params=limit,
        name="near",
    )(own, shift(to_next, 1), shift(to_last, -1), shift(to_right, 2), shift(to_left, -2))
    near, piece = lax.optimization_barrier((near, incoming[:, : tokens // 2]))
    pieces = [piece]
    for turn in (1, 2, 3):
        pieces.append(lax.ppermute(piece, "expert", [(i, i ^ turn) for i in range(groups)]))
    distant = lax.all_to_all(
        near,
        "dp",
        split_axis=0,
        concat_axis=0,
        tiled=True,
        axis_index_groups=far_groups,
    )
    own = total(distant)
    full = lax.all_gather(own, "dp", axis=1, tiled=True, axis_index_groups=far_groups)
    full = lax.all_gather(full, "dp", axis=0, tiled=True, axis_index_groups=near_groups)

    grad_pre, payload, shared_back = pl.pallas_call(
        lambda *refs: middle_kernel(capacity, *refs),
        out_shape=(
            pltpu.HBM((slots, 2 * hidden_width), jnp.bfloat16),
            jax.ShapeDtypeStruct((groups, tokens + 2 * SLOT_ROWS, LANES), jnp.bfloat16),
            jax.ShapeDtypeStruct((tokens, width), jnp.float32),
        ),
        in_specs=vmem(4) + [pl.BlockSpec(memory_space=pltpu.HBM)],
        out_specs=[pl.BlockSpec(memory_space=pltpu.HBM)] + vmem(2),
        scratch_shapes=[
            pltpu.VMEM(shared_gate_up.shape, jnp.bfloat16),
            pltpu.VMEM((slots, 2 * hidden_width), jnp.bfloat16),
            pltpu.SemaphoreType.DMA((2,)),
        ],
        compiler_params=limit,
        name="middle",
    )(full, routed_pre, shared_pre, w_gate_up, in_hbm(shared_gate_up))
    back = lax.all_to_all(payload, "expert", split_axis=0, concat_axis=0, tiled=True)

    gate = routed_pre[:, :hidden_width].astype(jnp.float32)
    up = routed_pre[:, hidden_width:].astype(jnp.float32)
    hidden = (gate * jax.nn.sigmoid(gate) * up).astype(jnp.bfloat16)
    grad_down = dot(hidden, arrived, 0, 0).astype(jnp.bfloat16)
    grad_gate_up = dot(routed_inputs, grad_pre, 0, 0).astype(jnp.bfloat16)

    gu_cols = 2 * hidden_width // groups
    down_cols = hidden_width // groups
    grad_in, shared_gu, shared_dn = pl.pallas_call(
        last_kernel,
        out_shape=(
            jax.ShapeDtypeStruct((tokens, width), jnp.bfloat16),
            jax.ShapeDtypeStruct((gu_cols, width), jnp.bfloat16),
            jax.ShapeDtypeStruct((down_cols, width), jnp.bfloat16),
        ),
        in_specs=[pl.BlockSpec(memory_space=pltpu.SMEM)]
        + vmem(3)
        + [pl.BlockSpec(memory_space=pltpu.HBM)] * 4,
        scratch_shapes=[
            pltpu.VMEM((4, *pieces[0].shape), jnp.bfloat16),
            pltpu.SemaphoreType.DMA((4,)),
        ],
        compiler_params=limit,
        name="last",
    )(turn_of, back, sel, shared_back, *[in_hbm(piece) for piece in pieces])
    return (
        grad_in,
        grad_gate_up[None],
        grad_down[None],
        shared_gu.T,
        shared_dn,
    )


def solution(mesh):
    in_specs = (
        P("expert", "dp"),
        P("expert", None),
        P("expert", None),
        P("expert", "dp"),
        P("expert", None),
        P("expert", None, "dp"),
        P("expert", None, None),
        P("expert", "dp", None),
        P("expert", None, "dp"),
        P("dp", None),
        P(None, "dp"),
    )
    out_specs = (
        P("expert", "dp"),
        P("expert", "dp", None),
        P("expert", None, "dp"),
        P("dp", "expert"),
        P("expert", "dp"),
    )
    return jax.shard_map(
        on_device, mesh=mesh, in_specs=in_specs, out_specs=out_specs, check_vma=False
    )
```

```python
import jax
import jax.numpy as jnp
from jax import lax
from jax.experimental import pallas as pl
from jax.experimental.pallas import tpu as pltpu
from jax.sharding import PartitionSpec as P

NEAR = 4


LANES = 128
SLOT_ROWS = 16


def in_hbm(x):
    return pltpu.with_memory_space_constraint(x, pltpu.HBM)


def vmem(count):
    return [pl.BlockSpec(memory_space=pltpu.VMEM) for _ in range(count)]


def dot(a, b, ca, cb):
    return lax.dot_general(a, b, (((ca,), (cb,)), ((), ())), preferred_element_type=jnp.float32)


def route_kernel(
    capacity,
    ids_hbm,
    gates_hbm,
    grad_hbm,
    inputs_hbm,
    sel_ref,
    out_ref,
    ids_ref,
    gates_ref,
    grad_ref,
    inputs_ref,
    sems,
):
    copies = [
        pltpu.make_async_copy(source, target, sems.at[i])
        for i, (source, target) in enumerate(
            (
                (ids_hbm, ids_ref),
                (gates_hbm, gates_ref),
                (grad_hbm, grad_ref),
                (inputs_hbm, inputs_ref),
            )
        )
    ]
    for copy in copies:
        copy.start()
    slots, tokens = sel_ref.shape
    slot = lax.broadcasted_iota(jnp.int32, (slots, 1), 0)
    expert = slot // SLOT_ROWS
    place = slot - expert * SLOT_ROWS
    place = jnp.where(place < capacity, place, tokens).astype(jnp.float32)
    for copy in copies:
        copy.wait()
    ids = ids_ref[...]
    gates = gates_ref[...]
    hit = jnp.zeros((slots, tokens), jnp.float32)
    weight = jnp.zeros((slots, tokens), jnp.float32)
    for k in range(ids.shape[0]):
        same = ids[k : k + 1, :] == expert
        hit = jnp.where(same, 1.0, hit)
        weight = jnp.where(same, gates[k : k + 1, :], weight)
    row = lax.broadcasted_iota(jnp.int32, (tokens, tokens), 0)
    col = lax.broadcasted_iota(jnp.int32, (tokens, tokens), 1)
    earlier = jnp.where(row < col, 1.0, 0.0).astype(jnp.bfloat16)
    rank = jnp.dot(hit.astype(jnp.bfloat16), earlier, preferred_element_type=jnp.float32)
    taken = (hit > 0.0) & (rank == place)
    sel = jnp.where(taken, 1.0, 0.0).astype(jnp.bfloat16)
    gate = jnp.sum(jnp.where(taken, weight, 0.0), axis=1, keepdims=True)
    rows = jnp.dot(sel, grad_ref[...], preferred_element_type=jnp.float32)
    sel_ref[...] = sel
    scaled = (gate * rows).reshape(slots // SLOT_ROWS, SLOT_ROWS, rows.shape[1])
    part = tokens // 2
    out_ref[:, part:, :] = scaled[:, :capacity, :].astype(jnp.bfloat16)
    for j in range(out_ref.shape[0]):
        source = grad_ref if j % 2 else inputs_ref
        at = j // 2 % 2 * part
        out_ref[j, :part, :] = source[at : at + part, :]


def part_kernel(
    at_ref,
    arrived_ref,
    grad_ref,
    w_ref,
    shared_w_ref,
    own_ref,
    next_ref,
    last_ref,
    left_ref,
    right_ref,
    blocks_ref,
):
    rows, columns = own_ref.shape
    routed = dot(arrived_ref[...], w_ref[...], 1, 0)
    shared = dot(grad_ref[...], shared_w_ref[...], 1, 0)
    both = jnp.concatenate([routed, shared], axis=0)
    for b in range(NEAR):
        blocks_ref[b] = both[b * rows : (b + 1) * rows].astype(jnp.bfloat16)
    at = at_ref[0]
    own_ref[...] = blocks_ref[at]
    next_ref[...] = blocks_ref[lax.rem(at + 1, NEAR)]
    last_ref[...] = blocks_ref[lax.rem(at + NEAR - 1, NEAR)]
    opposite = lax.rem(at + 2, NEAR)
    left_ref[...] = blocks_ref[opposite, :, : columns // 2]
    right_ref[...] = blocks_ref[opposite, :, columns // 2 :]


def near_kernel(own_ref, after_ref, before_ref, ahead_ref, behind_ref, out_ref):
    far, _, cols = out_ref.shape
    f32 = jnp.float32
    for a in range(far):
        lanes = slice(a * cols, (a + 1) * cols)
        total = own_ref[:, lanes].astype(f32) + after_ref[:, lanes].astype(f32)
        total = total + before_ref[:, lanes].astype(f32)
        half = ahead_ref if a < far // 2 else behind_ref
        at = a % (far // 2) * cols
        out_ref[a] = (total + half[:, at : at + cols].astype(f32)).astype(jnp.bfloat16)


def swiglu_terms(gate, up, grad_hidden):
    sig = jax.nn.sigmoid(gate)
    act = gate * sig
    return grad_hidden * up * sig * (1.0 + gate * (1.0 - sig)), grad_hidden * act, act * up


def middle_kernel(
    full_ref,
    routed_pre_ref,
    shared_pre_ref,
    w_ref,
    spread_ref,
    shared_w_hbm,
    grad_pre_hbm,
    payload_ref,
    shared_back_ref,
    shared_w_ref,
    grad_pre_ref,
    sems,
):
    shared_in = pltpu.make_async_copy(shared_w_hbm, shared_w_ref, sems.at[0])
    shared_in.start()
    slots = routed_pre_ref.shape[0]
    tokens = shared_pre_ref.shape[0]
    half = full_ref.shape[1]
    width = w_ref.shape[0]
    groups = payload_ref.shape[0]
    step = 16
    for r in range(0, slots, step):
        for c in range(0, half, half // 2):
            part = half // 2
            d_gate, d_up, _ = swiglu_terms(
                routed_pre_ref[r : r + step, c : c + part].astype(jnp.float32),
                routed_pre_ref[r : r + step, half + c : half + c + part].astype(jnp.float32),
                full_ref[r : r + step, c : c + part].astype(jnp.float32),
            )
            grad_pre_ref[r : r + step, c : c + part] = d_gate.astype(jnp.bfloat16)
            grad_pre_ref[r : r + step, half + c : half + c + part] = d_up.astype(jnp.bfloat16)
    grad_pre_out = pltpu.make_async_copy(grad_pre_ref, grad_pre_hbm, sems.at[1])
    grad_pre_out.start()
    d_gate, d_up, value = swiglu_terms(
        shared_pre_ref[:, :half].astype(jnp.float32),
        shared_pre_ref[:, half:].astype(jnp.float32),
        full_ref[slots:, :].astype(jnp.float32),
    )
    d_gate, d_up = d_gate.astype(jnp.bfloat16), d_up.astype(jnp.bfloat16)
    value = value.astype(jnp.bfloat16)
    shared_in.wait()
    shared_back_ref[...] = dot(d_gate, shared_w_ref[:, :half], 1, 1) + dot(
        d_up, shared_w_ref[:, half:], 1, 1
    )
    gu_cols, down_cols = 2 * half // groups, half // groups
    for j in range(groups):
        source = d_gate if j < groups // 2 else d_up
        at = j % (groups // 2) * gu_cols
        payload_ref[j, :tokens, :gu_cols] = source[:, at : at + gu_cols]
        payload_ref[j, :tokens, gu_cols : gu_cols + down_cols] = value[
            :, j * down_cols : (j + 1) * down_cols
        ]
    used = gu_cols + down_cols
    payload_ref[:, :tokens, used:] = jnp.zeros((groups, tokens, LANES - used), jnp.bfloat16)
    returned = dot(grad_pre_ref[...], w_ref[...], 1, 1).astype(jnp.bfloat16)
    spaced = dot(spread_ref[...], returned, 1, 0).astype(jnp.bfloat16)
    spaced = spaced.reshape(groups, SLOT_ROWS, width)
    payload_ref[:, tokens : tokens + SLOT_ROWS, :] = spaced[:, :, :LANES]
    payload_ref[:, tokens + SLOT_ROWS :, : width - LANES] = spaced[:, :, LANES:]
    payload_ref[:, tokens + SLOT_ROWS :, width - LANES :] = jnp.zeros(
        (groups, SLOT_ROWS, 2 * LANES - width), jnp.bfloat16
    )
    grad_pre_out.wait()


def last_kernel(
    turn_ref,
    back_ref,
    sel_ref,
    shared_back_ref,
    first_hbm,
    second_hbm,
    third_hbm,
    fourth_hbm,
    grad_in_ref,
    shared_gu_ref,
    shared_dn_ref,
    pieces_ref,
    sems,
):
    copies = [
        pltpu.make_async_copy(source, pieces_ref.at[i], sems.at[i])
        for i, source in enumerate((first_hbm, second_hbm, third_hbm, fourth_hbm))
    ]
    for copy in copies:
        copy.start()
    groups = back_ref.shape[0]
    slots, tokens = sel_ref.shape
    gu_cols, width = shared_gu_ref.shape
    down_cols = shared_dn_ref.shape[0]
    low = back_ref[:, tokens : tokens + SLOT_ROWS, :].reshape(slots, LANES)
    high = back_ref[:, tokens + SLOT_ROWS :, :].reshape(slots, LANES)
    sel = sel_ref[...]
    shared_back = shared_back_ref[...]
    grad_in_ref[:, :LANES] = (shared_back[:, :LANES] + dot(sel, low, 0, 0)).astype(jnp.bfloat16)
    grad_in_ref[:, LANES:] = (
        shared_back[:, LANES:] + dot(sel, high, 0, 0)[:, : width - LANES]
    ).astype(jnp.bfloat16)
    for copy in copies:
        copy.wait()
    part = tokens // 2
    shared_gu = jnp.zeros((LANES, width), jnp.float32)
    shared_dn = jnp.zeros((LANES, width), jnp.float32)
    for h in range(2):
        shared = back_ref[:, h * part : (h + 1) * part, :].reshape(groups * part, LANES).T
        inputs = pieces_ref[jnp.bitwise_xor(turn_ref[0], 2 * h)].reshape(groups * part, width)
        grads = pieces_ref[jnp.bitwise_xor(turn_ref[0], 2 * h + 1)].reshape(groups * part, width)
        shared_gu = shared_gu + dot(shared, inputs, 1, 0)
        shared_dn = shared_dn + dot(shared, grads, 1, 0)
    shared_gu_ref[...] = shared_gu[:gu_cols].astype(jnp.bfloat16)
    shared_dn_ref[...] = shared_dn[gu_cols : gu_cols + down_cols].astype(jnp.bfloat16)


def total(parts):
    acc = parts[0].astype(jnp.float32)
    for i in range(1, parts.shape[0]):
        acc = acc + parts[i].astype(jnp.float32)
    return acc.astype(jnp.bfloat16)


def on_device(
    grad_out,
    expert_ids,
    gate_weights,
    layer_inputs,
    shared_pre,
    routed_inputs,
    routed_pre,
    w_gate_up,
    w_down,
    shared_gate_up,
    shared_down,
):
    groups = lax.axis_size("expert")
    ring = lax.axis_size("dp")
    far = ring // NEAR
    near_groups = [[NEAR * a + b for b in range(NEAR)] for a in range(far)]
    far_groups = [[NEAR * a + b for a in range(far)] for b in range(NEAR)]
    slots = routed_pre.shape[1]
    capacity = slots // groups
    tokens, width = grad_out.shape
    hidden_width = w_down.shape[1]
    routed_pre, routed_inputs = routed_pre[0], routed_inputs[0]
    w_gate_up, w_down = w_gate_up[0], w_down[0]

    limit = pltpu.CompilerParams(vmem_limit_bytes=16 * 1024 * 1024)
    sel, outgoing = pl.pallas_call(
        lambda *refs: route_kernel(capacity, *refs),
        out_shape=(
            jax.ShapeDtypeStruct((groups * SLOT_ROWS, tokens), jnp.bfloat16),
            jax.ShapeDtypeStruct((groups, tokens // 2 + capacity, width), jnp.bfloat16),
        ),
        in_specs=[pl.BlockSpec(memory_space=pltpu.HBM)] * 4,
        scratch_shapes=[
            pltpu.VMEM(expert_ids.shape[::-1], jnp.int32),
            pltpu.VMEM(gate_weights.shape[::-1], jnp.float32),
            pltpu.VMEM(grad_out.shape, jnp.bfloat16),
            pltpu.VMEM(layer_inputs.shape, jnp.bfloat16),
            pltpu.SemaphoreType.DMA((4,)),
        ],
        compiler_params=limit,
        name="route",
    )(*[in_hbm(x) for x in (expert_ids.T, gate_weights.T, grad_out, layer_inputs)])
    incoming = lax.all_to_all(outgoing, "expert", split_axis=0, concat_axis=0, tiled=True)
    arrived = incoming[:, tokens // 2 :].reshape(slots, width)
    turn_of = (lax.axis_index("expert") % 4).reshape(1).astype(jnp.int32)

    rows = (slots + tokens) // NEAR
    cols = hidden_width // far
    half = hidden_width // 2

    def shift(x, by):
        return lax.ppermute(x, "dp", [(i, (i + by) % ring) for i in range(ring)])

    def block(columns):
        return jax.ShapeDtypeStruct((rows, columns), jnp.bfloat16)

    quarter = (lax.axis_index("dp") % NEAR).reshape(1).astype(jnp.int32)
    own, to_next, to_last, to_right, to_left = pl.pallas_call(
        part_kernel,
        out_shape=(block(hidden_width),) * 3 + (block(half),) * 2,
        in_specs=[pl.BlockSpec(memory_space=pltpu.SMEM)] + vmem(4),
        out_specs=vmem(5),
        scratch_shapes=[pltpu.VMEM((NEAR, rows, hidden_width), jnp.bfloat16)],
        compiler_params=limit,
        name="part",
    )(quarter, arrived, grad_out, w_down.T, shared_down.T)
    near = pl.pallas_call(
        near_kernel,
        out_shape=jax.ShapeDtypeStruct((far, rows, cols), jnp.bfloat16),
        in_specs=vmem(5),
        out_specs=vmem(1)[0],
        compiler_params=limit,
        name="near",
    )(own, shift(to_next, 1), shift(to_last, -1), shift(to_right, 2), shift(to_left, -2))
    place = jnp.arange(groups * SLOT_ROWS, dtype=jnp.int32)
    place = jnp.where(
        place % SLOT_ROWS < capacity, place // SLOT_ROWS * capacity + place % SLOT_ROWS, -1
    )
    near, piece, place = lax.optimization_barrier((near, incoming[:, : tokens // 2], place))
    spread = (place[:, None] == jnp.arange(slots, dtype=jnp.int32)[None]).astype(jnp.bfloat16)
    pieces = [piece]
    for turn in (1, 2, 3):
        pieces.append(lax.ppermute(piece, "expert", [(i, i ^ turn) for i in range(groups)]))
    distant = lax.all_to_all(
        near,
        "dp",
        split_axis=0,
        concat_axis=0,
        tiled=True,
        axis_index_groups=far_groups,
    )
    own = total(distant)
    full = lax.all_gather(own, "dp", axis=1, tiled=True, axis_index_groups=far_groups)
    full = lax.all_gather(full, "dp", axis=0, tiled=True, axis_index_groups=near_groups)

    grad_pre, payload, shared_back = pl.pallas_call(
        middle_kernel,
        out_shape=(
            pltpu.HBM((slots, 2 * hidden_width), jnp.bfloat16),
            pltpu.HBM((groups, tokens + 2 * SLOT_ROWS, LANES), jnp.bfloat16),
            jax.ShapeDtypeStruct((tokens, width), jnp.float32),
        ),
        in_specs=vmem(5) + [pl.BlockSpec(memory_space=pltpu.HBM)],
        out_specs=[pl.BlockSpec(memory_space=pltpu.HBM), pl.BlockSpec(), *vmem(1)],
        scratch_shapes=[
            pltpu.VMEM(shared_gate_up.shape, jnp.bfloat16),
            pltpu.VMEM((slots, 2 * hidden_width), jnp.bfloat16),
            pltpu.SemaphoreType.DMA((2,)),
        ],
        compiler_params=limit,
        name="middle",
    )(full, routed_pre, shared_pre, w_gate_up, spread, in_hbm(shared_gate_up))
    back = lax.all_to_all(payload, "expert", split_axis=0, concat_axis=0, tiled=True)

    gate = routed_pre[:, :hidden_width].astype(jnp.float32)
    up = routed_pre[:, hidden_width:].astype(jnp.float32)
    hidden = (gate * jax.nn.sigmoid(gate) * up).astype(jnp.bfloat16)
    grad_down = dot(hidden, arrived, 0, 0).astype(jnp.bfloat16)
    grad_gate_up = dot(routed_inputs, grad_pre, 0, 0).astype(jnp.bfloat16)

    gu_cols = 2 * hidden_width // groups
    down_cols = hidden_width // groups
    grad_in, shared_gu, shared_dn = pl.pallas_call(
        last_kernel,
        out_shape=(
            jax.ShapeDtypeStruct((tokens, width), jnp.bfloat16),
            jax.ShapeDtypeStruct((gu_cols, width), jnp.bfloat16),
            jax.ShapeDtypeStruct((down_cols, width), jnp.bfloat16),
        ),
        in_specs=[pl.BlockSpec(memory_space=pltpu.SMEM)]
        + vmem(3)
        + [pl.BlockSpec(memory_space=pltpu.HBM)] * 4,
        scratch_shapes=[
            pltpu.VMEM((4, *pieces[0].shape), jnp.bfloat16),
            pltpu.SemaphoreType.DMA((4,)),
        ],
        compiler_params=limit,
        name="last",
    )(turn_of, back, sel, shared_back, *[in_hbm(piece) for piece in pieces])
    return (
        grad_in,
        grad_gate_up[None],
        grad_down[None],
        shared_gu.T,
        shared_dn,
    )


def solution(mesh):
    in_specs = (
        P("expert", "dp"),
        P("expert", None),
        P("expert", None),
        P("expert", "dp"),
        P("expert", None),
        P("expert", None, "dp"),
        P("expert", None, None),
        P("expert", "dp", None),
        P("expert", None, "dp"),
        P("dp", None),
        P(None, "dp"),
    )
    out_specs = (
        P("expert", "dp"),
        P("expert", "dp", None),
        P("expert", None, "dp"),
        P("dp", "expert"),
        P("expert", "dp"),
    )
    return jax.shard_map(
        on_device, mesh=mesh, in_specs=in_specs, out_specs=out_specs, check_vma=False
    )
```
